256 devices in a mesh: band: 64 (over x, z_lo, y, core), img: 4 (over z_hi).
Axes of the slice: x: 4, y: 4, z: 8 (z_hi: 4, z_lo: 2; z = z_hi * 2 + z_lo), core: 2. Of those that a mesh axis runs over, the one named last changes fastest.
Arguments:
- latent: bfloat16 [512, 128, 640], P(('img', 'band')), parts along dimension 0, may hold values from -27 to 27
- gn_gain: float32 [640], replicated, may hold values from 0.25 to 1.75
- gn_bias: float32 [640], replicated, may hold values from -3 to 3
- conv_weight: bfloat16 [3, 3, 640, 640], replicated, may hold values from -0.15625 to 0.15625
- conv_bias: float32 [640], replicated, may hold values from -3 to 3
- ln_gain: float32 [640], replicated, may hold values from 0.5 to 3.5
- ln_bias: float32 [640], replicated, may hold values from -2 to 2
- w_query: bfloat16 [640, 640], replicated, may hold values from -4 to 4
- w_key: bfloat16 [640, 640], replicated, may hold values from -4 to 4
- w_value: bfloat16 [640, 640], replicated, may hold values from -4 to 4
Outputs:
- result: bfloat16 [512, 128, 640], P(('img', 'band')), parts along dimension 0
The draws below stay inside these ranges and needn't reach their ends.
There are 4 independent parts, one for each index of `img`. The reference program is written for one: setup_inputs(seed, part) draws one part's arguments, and reference() takes and returns one part's arrays. A program takes and returns all parts, laid end to end along the dimension named above; an argument that names none is the same for every part. Nothing has to cross between parts.
All inputs are finite; a program needn't handle non-finite values.
Results may differ from the reference program's by a relative error of at most 0.015.
Values may be sent and summed in bfloat16 or wider, within the bound.
No kernel may reach another device: no remote copies, remote signals or barrier semaphores. Data moves between devices by JAX's collectives and lax.ppermute only.
A program may use at most 128 MiB of HBM per device.

```python
import math
import jax
import jax.numpy as jnp
from jax import lax

C = 640
HEAD_DIM = 64
HEADS = 10
GROUPS = 16
COLS = 128
ROWS = 128
TOKENS = 16384


def pattern_sign():
    chan = jnp.arange(C)
    return (1 - 2 * ((chan + chan // 3) % 2)).astype(jnp.float32)


def shared_vector(key):
    return jnp.clip(jax.random.normal(key, (C,), jnp.float32), -3.0, 3.0)


def row_profile(key):
    first, second, third, fourth = jax.random.split(key, 4)
    spot = jnp.arange(ROWS).astype(jnp.float32) / ROWS
    freq = jax.random.uniform(first, (2,), jnp.float32, 0.5, 2.0)
    phase = jax.random.uniform(second, (2,), jnp.float32, 0.0, 2.0 * math.pi)
    amplitude = jax.random.uniform(third, (2,), jnp.float32, 0.25, 0.4)
    wave = jnp.sum(amplitude[None, :] * jnp.sin(2.0 * math.pi * freq[None, :] * spot[:, None] + phase[None, :]), axis=1)
    jitter = jax.random.uniform(fourth, (ROWS,), jnp.float32, -0.4, 0.4)
    level = jnp.log(3.0) * spot - 0.4 + wave + jitter
    level = jnp.clip(level, math.log(0.4), math.log(3.3))
    return jnp.exp(level)[:, None, None]


def draw_latent(key, part):
    key = jax.random.fold_in(key, 11)
    first = jax.random.fold_in(key, 0)
    second = jax.random.fold_in(key, 1)
    sixth = jax.random.fold_in(key, 5)
    row_scale = row_profile(second)
    amount = jax.random.uniform(sixth, (ROWS, COLS, 1), jnp.float32, -1.0, 2.0)
    base = jnp.clip(jax.random.normal(first, (ROWS, COLS, C), jnp.float32), -6.0, 6.0)
    base = base + amount * pattern_sign()
    result = base * row_scale
    return result.astype(jnp.bfloat16)


def draw_ln_gain(key, part):
    key = jax.random.fold_in(key, 12)
    return jax.random.uniform(key, (C,), jnp.float32, 1.2, 2.5)


def draw_w_query(key, part):
    common = shared_vector(key)
    key = jax.random.fold_in(key, 13)
    own = jnp.clip(jax.random.normal(key, (C, C), jnp.float32), -4.0, 4.0)
    own = own + 0.6 * pattern_sign()[:, None] * common[None, :] / jnp.sqrt(jnp.float32(C))
    return (own / jnp.sqrt(jnp.float32(C))).astype(jnp.bfloat16)


def draw_w_key(key, part):
    common = shared_vector(key)
    key = jax.random.fold_in(key, 14)
    own = jnp.clip(jax.random.normal(key, (C, C), jnp.float32), -4.0, 4.0)
    own = own + 0.6 * pattern_sign()[:, None] * common[None, :] / jnp.sqrt(jnp.float32(C))
    return (own / jnp.sqrt(jnp.float32(C))).astype(jnp.bfloat16)


def draw_w_value(key, part):
    key = jax.random.fold_in(key, 15)
    first, second = jax.random.split(key)
    own = jnp.clip(jax.random.normal(first, (C, C), jnp.float32), -4.0, 4.0)
    direction = jnp.clip(jax.random.normal(second, (C,), jnp.float32), -3.0, 3.0)
    own = own + pattern_sign()[:, None] * direction[None, :] / jnp.sqrt(jnp.float32(C))
    return (own / jnp.sqrt(jnp.float32(C))).astype(jnp.bfloat16)


def bell_draw(key, extent, deviation, reach, kind=jnp.bfloat16):
    return jnp.clip(deviation * jax.random.normal(key, extent, jnp.float32), -reach, reach).astype(kind)


def setup_inputs(seed: int = 0, part: int = 0) -> dict:
    keys = jax.random.split(jax.random.key(seed), 11)
    own_keys = jax.random.split(jax.random.fold_in(keys[10], part), 11)
    latent = draw_latent(jax.random.fold_in(jax.random.fold_in(keys[10], part), 71), part)
    gn_gain = jnp.clip(1.0 + 0.15 * jax.random.normal(keys[1], (C,), jnp.float32), 0.25, 1.75)
    gn_bias = bell_draw(keys[2], (C,), 0.5, 3.0, jnp.float32)
    conv_weight = bell_draw(keys[3], (3, 3, C, C), (9 * C // 4) ** -0.5, 0.15625)
    conv_bias = bell_draw(keys[4], (C,), 0.5, 3.0, jnp.float32)
    ln_gain = draw_ln_gain(jax.random.fold_in(keys[10], 71), part)
    ln_bias = bell_draw(keys[6], (C,), 0.3, 2.0, jnp.float32)
    w_query = draw_w_query(jax.random.fold_in(keys[10], 71), part)
    w_key = draw_w_key(jax.random.fold_in(keys[10], 71), part)
    w_value = draw_w_value(jax.random.fold_in(keys[10], 71), part)
    return dict(latent=latent, gn_gain=gn_gain, gn_bias=gn_bias, conv_weight=conv_weight, conv_bias=conv_bias, ln_gain=ln_gain, ln_bias=ln_bias, w_query=w_query, w_key=w_key, w_value=w_value)


def norm_act(latent, gn_gain, gn_bias):
    width = C // GROUPS
    flat = latent.astype(jnp.float32).reshape(-1, GROUPS, width)
    count = flat.shape[0] * width
    mean = lax.optimization_barrier(jnp.sum(flat, axis=(0, 2))) / count
    meansq = lax.optimization_barrier(jnp.sum(flat * flat, axis=(0, 2))) / count
    var = meansq - mean * mean
    normed = (flat - mean[None, :, None]) * lax.rsqrt(var + 1e-05)[None, :, None]
    value = normed.reshape(-1, C) * gn_gain + gn_bias
    return jax.nn.silu(value).astype(jnp.bfloat16).reshape(latent.shape)

def layer_norm(hidden, ln_gain, ln_bias):
    values = hidden.astype(jnp.float32)
    centre = lax.optimization_barrier(jnp.mean(values, axis=-1, keepdims=True))
    spread = lax.optimization_barrier(jnp.mean((values - centre) ** 2, axis=-1, keepdims=True))
    return ((values - centre) * lax.rsqrt(spread + 1e-05) * ln_gain + ln_bias).astype(jnp.bfloat16)

def reference(latent, gn_gain, gn_bias, conv_weight, conv_bias, ln_gain, ln_bias, w_query, w_key, w_value):
    act = norm_act(latent, gn_gain, gn_bias)
    padded = jnp.pad(act, ((1, 1), (1, 1), (0, 0)))
    total = latent.astype(jnp.float32).reshape(-1, C) + conv_bias
    for row_off in range(3):
        for col_off in range(3):
            window = padded[row_off:row_off + ROWS, col_off:col_off + COLS].reshape(-1, C)
            total = total + jnp.dot(window, conv_weight[row_off, col_off], preferred_element_type=jnp.float32)
    hidden = total.astype(jnp.bfloat16)
    normed = layer_norm(hidden, ln_gain, ln_bias)
    query = jnp.dot(normed, w_query, preferred_element_type=jnp.float32).astype(jnp.bfloat16)
    key = jnp.dot(normed, w_key, preferred_element_type=jnp.float32).astype(jnp.bfloat16)
    value = jnp.dot(normed, w_value, preferred_element_type=jnp.float32).astype(jnp.bfloat16)
    count = TOKENS
    block = math.gcd(count, 1024)
    scale = 1.0 / math.sqrt(HEAD_DIM)
    q_heads = query.reshape(count, HEADS, HEAD_DIM).transpose(1, 0, 2)
    k_heads = key.reshape(count, HEADS, HEAD_DIM).transpose(1, 0, 2)
    v_heads = value.reshape(count, HEADS, HEAD_DIM).transpose(1, 0, 2)

    def one_head(parts):
        q_one, k_one, v_one = parts

        def one_block(q_block):
            score = jnp.dot(q_block, k_one.T, preferred_element_type=jnp.float32) * scale
            top = lax.optimization_barrier(jnp.max(score, axis=-1, keepdims=True))
            weights = jnp.exp(score - top)
            denom = lax.optimization_barrier(jnp.sum(weights, axis=-1, keepdims=True))
            return jnp.dot(weights.astype(jnp.bfloat16), v_one, preferred_element_type=jnp.float32) / denom
        outs = lax.map(one_block, q_one.reshape(count // block, block, HEAD_DIM))
        return outs.reshape(count, HEAD_DIM)
    attended = lax.map(one_head, (q_heads, k_heads, v_heads))
    attended = attended.transpose(1, 0, 2).reshape(count, C)
    result = (hidden.astype(jnp.float32) + attended).astype(jnp.bfloat16)
    return result.reshape(ROWS, COLS, C)
```

```python
import functools
import math

import jax
import jax.numpy as jnp
from jax import lax
from jax.experimental import pallas as pl
from jax.experimental.pallas import tpu as pltpu
from jax.sharding import Mesh
from jax.sharding import PartitionSpec as P

HEADS = 10
HEAD_DIM = 64
GROUPS = 16
NX, NZ, NY, NC = (4, 2, 4, 2)
BAND = ("x", "z", "y", "core")
RING = ("y", "core")
SETS = NX * NZ
BANDS = NX * NZ * NY * NC
TILE = 512
TILES = 4
LANES = 128
Q_ROWS = 256
KV_ROWS = 320
SEND_ROWS = Q_ROWS + KV_ROWS
BACK_ROWS = 272
HIGH = 2.0**100
LOW = 2.0**-60
BF16 = jnp.bfloat16
F32 = jnp.float32
VMEM = pltpu.CompilerParams(vmem_limit_bytes=24 * 1024 * 1024)


def total_of(value):
    for axis, size in (("y", NY), (("z", "core"), NZ * NC), ("x", NX)):
        parts = [value]
        for step in range(1, size):
            perm = [(i, (i + step) % size) for i in range(size)]
            parts.append(lax.ppermute(value, axis, perm))
        value = sum(parts[1:], parts[0])
    return value


def halo(latent):
    up = [(i, i + 1) for i in range(BANDS - 1)]
    down = [(j, i) for i, j in up]
    before = lax.ppermute(latent[-1:], BAND, up)
    after = lax.ppermute(latent[:1], BAND, down)
    return before, after


def dot(a, b):
    return jnp.dot(a, b, preferred_element_type=F32)


def swap(a):
    return jnp.concatenate([a[:, 64:128], a[:, 0:64]], axis=1)


def lanes(rows):
    return lax.broadcasted_iota(jnp.int32, (rows, LANES), 1)


def front_kernel(
    sums_ref, vec_ref, before_ref, after_ref, latent_hbm, conv_hbm, wq_hbm, wk_hbm, wv_hbm,
    hidden_ref, send_ref, shift_ref, latent_ref, conv_ref, w_ref, sems,
):
    copies = [pltpu.make_async_copy(latent_hbm, latent_ref, sems.at[0])]
    for i in range(3):
        copies.append(pltpu.make_async_copy(conv_hbm.at[i], conv_ref.at[i], sems.at[1 + i]))
    for i, w_hbm in enumerate((wq_hbm, wk_hbm, wv_hbm)):
        copies.append(pltpu.make_async_copy(w_hbm, w_ref.at[i], sems.at[4 + i]))
    for copy in copies:
        copy.start()
    chans = latent_ref.shape[2]
    count = float(BANDS * 256 * (chans // GROUPS))
    mean = sums_ref[0:1] / count
    var = sums_ref[1:2] / count - mean * mean
    rate = lax.rsqrt(var + 1e-05)
    gain, bias = vec_ref[0:1], vec_ref[1:2]
    row = lax.broadcasted_iota(jnp.int32, (128, chans), 0)
    copies[0].wait()
    sources = [before_ref[0], latent_ref[0], latent_ref[1], after_ref[0]]
    for r, source in enumerate(sources):
        value = (source.astype(F32) - mean) * rate * gain + bias
        act = value / (1.0 + jnp.exp(-value))
        if r == 0:
            act = act * vec_ref[5:6]
        if r == 3:
            act = act * vec_ref[6:7]
        here = slice(128 * r, 128 * r + 128)
        left = jnp.where(row == 0, 0.0, pltpu.roll(act, 1, 0))
        right = jnp.where(row == 127, 0.0, pltpu.roll(act, 127, 0))
        shift_ref[0, here] = left.astype(BF16)
        shift_ref[1, here] = act.astype(BF16)
        shift_ref[2, here] = right.astype(BF16)
    total = latent_ref[...].reshape(256, chans).astype(F32) + vec_ref[2:3]
    for i in range(3):
        copies[1 + i].wait()
        for col in range(3):
            total = total + dot(shift_ref[col, 128 * i : 128 * i + 256, :], conv_ref[i, col])
    hidden = total.astype(BF16)
    hidden_ref[...] = hidden
    values = hidden.astype(F32)
    values = values - jnp.mean(values, axis=1, keepdims=True)
    spread = jnp.mean(values * values, axis=1, keepdims=True)
    normed = (values * lax.rsqrt(spread + 1e-05) * vec_ref[3:4] + vec_ref[4:5]).astype(BF16)
    scale = math.log2(math.e) / math.sqrt(HEAD_DIM)
    copies[4].wait()
    query = (dot(normed, w_ref[0]) * scale).astype(BF16)
    copies[5].wait()
    key = dot(normed, w_ref[1]).T.astype(BF16)
    copies[6].wait()
    value = dot(normed, w_ref[2]).astype(BF16)
    for s in range(SETS):
        main, extra, part = 64 * s, 64 * (SETS + s // 4), 64 * (s % 4)
        send_ref[s, 0:256] = jnp.concatenate(
            [query[:, main : main + 64], query[:, extra : extra + 64]], axis=1
        )
        send_ref[s, 256:320] = key[main : main + 64, 0:128]
        send_ref[s, 320:384] = key[main : main + 64, 128:256]
        send_ref[s, 384:512] = jnp.concatenate(
            [value[0:128, main : main + 64], value[128:256, main : main + 64]], axis=1
        )
        send_ref[s, 512:576] = jnp.concatenate(
            [key[extra : extra + 64, part : part + 64], value[part : part + 64, extra : extra + 64]],
            axis=1,
        )


def front(sums, vec, before, after, latent, conv_weight, w_query, w_key, w_value):
    chans = latent.shape[2]
    far = [latent, conv_weight, w_query, w_key, w_value]
    far = [pltpu.with_memory_space_constraint(a, pltpu.HBM) for a in far]
    return pl.pallas_call(
        front_kernel,
        in_specs=[pl.BlockSpec(memory_space=pltpu.VMEM)] * 4
        + [pl.BlockSpec(memory_space=pltpu.HBM)] * 5,
        out_specs=[pl.BlockSpec(memory_space=pltpu.VMEM)] * 2,
        out_shape=[
            jax.ShapeDtypeStruct((256, chans), BF16),
            jax.ShapeDtypeStruct((SETS, SEND_ROWS, LANES), BF16),
        ],
        scratch_shapes=[
            pltpu.VMEM((3, 512, chans), BF16),
            pltpu.VMEM(latent.shape, BF16),
            pltpu.VMEM(conv_weight.shape, BF16),
            pltpu.VMEM((3, chans, chans), BF16),
            pltpu.SemaphoreType.DMA((7,)),
        ],
        compiler_params=VMEM,
        name="front",
    )(sums, vec, before, after, *far)


def main_step(kv_ref, pair):
    lane = lanes(128)
    keys, values = [], []
    for src in (2 * pair, 2 * pair + 1):
        keys += [kv_ref[src, 0:64, :], kv_ref[src, 64:128, :]]
        value = kv_ref[src, 128:256, :]
        for side in (value, swap(value)):
            values.append(jnp.where(lane < 64, side, jnp.ones_like(side)))
    keys = jnp.concatenate([jnp.concatenate(keys, axis=1), jnp.zeros((64, TILE), BF16)], axis=0)
    return 0, keys, jnp.concatenate(values, axis=0)


def extra_step(kv_ref, block):
    lane = lanes(64)
    sources = [SETS * block + src for src in range(SETS)]
    keys = [kv_ref[src, 256:320, 0:64] for src in sources]
    values = [kv_ref[src, 256:320, :] for src in sources]
    values = [jnp.where(lane >= 64, v, jnp.ones_like(v)) for v in values]
    keys = jnp.concatenate([jnp.zeros((64, TILE), BF16), jnp.concatenate(keys, axis=1)], axis=0)
    return 1, keys, jnp.concatenate(values, axis=0)


def fold_kernel(count, first, last, q_ref, *refs):
    kv_refs, refs = refs[:count], refs[count:]
    if not first:
        acc_in, refs = refs[0], refs[1:]
    if last:
        far_refs, refs = refs[:SETS], refs[SETS:]
    acc_ref = refs[0]
    acc_ref[0] = jnp.zeros((2, TILE, LANES), F32) if first else acc_in[0]
    query = q_ref[...].reshape(TILE, LANES)

    steps = []
    for kv_ref in kv_refs:
        steps += [functools.partial(main_step, kv_ref, pair) for pair in range(SETS // 2)]
        steps.append(functools.partial(extra_step, kv_ref, 0))
    held = None
    for step in steps + [None]:
        if step is not None:
            kind, keys, values = step()
            score = dot(query, keys)
        if held is not None:
            held_kind, held_score, held_values = held
            weight = jnp.exp2(held_score).astype(BF16)
            acc_ref[0, held_kind] += dot(weight, held_values)
        held = None if step is None else (kind, score, values)

    if last:
        out_ref, store_ref, top_ref, sems = refs[1:]
        wide = lanes(TILE)
        total = jnp.where(wide < 64, acc_ref[0, 1], acc_ref[0, 0])
        good = (jnp.min(total) > LOW) & (jnp.max(total) < HIGH)
        top_ref[...] = jnp.zeros((2, TILE, LANES), F32)

        @pl.when(jnp.logical_not(good))
        def _():
            copies = []
            for i, far_ref in enumerate(far_refs):
                here = store_ref.at[pl.ds(SETS * i, SETS)]
                copies.append(pltpu.make_async_copy(far_ref, here, sems.at[i]))
                copies[-1].start()
            acc_ref[0] = jnp.zeros((2, TILE, LANES), F32)
            top_ref[...] = jnp.full((2, TILE, LANES), -1e30, F32)
            for copy in copies:
                copy.wait()

            def online(step):
                kind, keys, values = step
                score = dot(query, keys)
                top = jnp.maximum(top_ref[kind], jnp.max(score, axis=1, keepdims=True))
                weight = jnp.exp2(score - top[:, 0:1]).astype(BF16)
                factor = jnp.exp2(top_ref[kind] - top)
                acc_ref[0, kind] = acc_ref[0, kind] * factor + dot(weight, values)
                top_ref[kind] = top

            def pair_body(pair, carry):
                online(main_step(store_ref, pair))
                return carry

            def block_body(block, carry):
                online(extra_step(store_ref, block))
                return carry

            lax.fori_loop(0, SETS * SETS // 2, pair_body, 0)
            lax.fori_loop(0, SETS, block_body, 0)

        main, extra = acc_ref[0, 0], acc_ref[0, 1]
        out = jnp.where(wide < 64, main / swap(main), extra / swap(extra)).astype(BF16)
        level = (jnp.log2(extra) + top_ref[1])[:, 0:1]
        row = lax.broadcasted_iota(jnp.int32, (16, LANES), 0)
        for src in range(2):
            out_ref[src, 0:256] = out[256 * src : 256 * src + 256]
            tail = jnp.zeros((16, LANES), F32)
            for half in range(2):
                base = 256 * src + 128 * half
                line = jnp.broadcast_to(level[base : base + 128], (128, LANES)).T[0:16]
                for part in range(3):
                    piece = line.astype(BF16).astype(F32)
                    tail = jnp.where(row == 2 * part + half, piece, tail)
                    line = line - piece
            out_ref[src, 256:272] = tail.astype(BF16)


def fold(got, blocks, acc, every=None):
    first, last = acc is None, every is not None
    acc_spec = pl.BlockSpec((1, 2, TILE, LANES), lambda t: (t, 0, 0, 0))
    kv_spec = pl.BlockSpec((SETS, KV_ROWS, LANES), lambda t: (0, 0, 0))
    out_specs = [acc_spec]
    out_shape = [jax.ShapeDtypeStruct((TILES, 2, TILE, LANES), F32)]
    scratch = []
    if last:
        out_specs.append(pl.BlockSpec((2, BACK_ROWS, LANES), lambda t: (t, 0, 0)))
        out_shape.append(jax.ShapeDtypeStruct((SETS, BACK_ROWS, LANES), BF16))
        scratch = [
            pltpu.VMEM((SETS * SETS, KV_ROWS, LANES), BF16),
            pltpu.VMEM((2, TILE, LANES), F32),
            pltpu.SemaphoreType.DMA((SETS,)),
        ]
    return pl.pallas_call(
        functools.partial(fold_kernel, len(blocks), first, last),
        grid=(TILES,),
        in_specs=[pl.BlockSpec((2, Q_ROWS, LANES), lambda t: (t, 0, 0))]
        + [kv_spec] * len(blocks)
        + ([] if first else [acc_spec])
        + ([pl.BlockSpec(memory_space=pl.ANY)] * SETS if last else []),
        out_specs=out_specs,
        out_shape=out_shape,
        scratch_shapes=scratch,
        input_output_aliases={} if first else {1 + len(blocks): 0},
        compiler_params=VMEM,
        name="fold",
    )(got, *blocks, *(() if first else (acc,)), *(every or ()))


def on_device(
    latent, gn_gain, gn_bias, conv_weight, conv_bias, ln_gain, ln_bias, w_query, w_key, w_value
):
    rows_here, cols, chans = latent.shape
    tokens = rows_here * cols
    width = chans // GROUPS
    before, after = halo(latent)
    flat = latent.astype(F32).reshape(-1, chans)
    sums = jnp.stack([jnp.sum(flat, axis=0), jnp.sum(flat * flat, axis=0)])
    sums = jnp.sum(sums.reshape(2, GROUPS, width), axis=2, keepdims=True)
    sums = total_of(jnp.broadcast_to(sums, (2, GROUPS, width)).reshape(2, chans))
    place = lax.axis_index(BAND)
    row = lax.broadcasted_iota(jnp.int32, (8, chans), 0)
    vec = jnp.where(row == 5, jnp.where(place > 0, 1.0, 0.0), 0.0)
    vec = jnp.where(row == 6, jnp.where(place < BANDS - 1, 1.0, 0.0), vec)
    for i, part in enumerate((gn_gain, gn_bias, conv_bias, ln_gain, ln_bias)):
        vec = jnp.where(row == i, part, vec)
    hidden, send = front(
        sums, vec, before, after, latent, conv_weight, w_query, w_key, w_value
    )

    got = lax.all_to_all(send, ("x", "z"), 0, 0)
    own = got[:, Q_ROWS:]
    spots = [(y, c) for y in range(NY) for c in range(NC)]
    along = [(2 * y + c, 2 * ((y + 1 - 2 * c) % NY) + c) for y, c in spots]
    against = [(j, i) for i, j in along]
    cross = [(2 * y + c, 2 * y + 1 - c) for y, c in spots]

    tied = lax.optimization_barrier
    twin = lax.ppermute(own, RING, cross)
    ahead = lax.ppermute(own, RING, along)
    (acc,) = fold(got, [own], None)
    own, acc = tied((own, acc))
    behind = lax.ppermute(own, RING, against)
    (acc,) = fold(got, [twin], acc)
    ahead, acc = tied((ahead, acc))
    ahead_twin = lax.ppermute(ahead, RING, cross)
    (acc,) = fold(got, [ahead], acc)
    ahead, acc = tied((ahead, acc))
    far = lax.ppermute(ahead, RING, along)
    (acc,) = fold(got, [behind], acc)
    behind, acc = tied((behind, acc))
    behind_twin = lax.ppermute(behind, RING, cross)
    (acc,) = fold(got, [ahead_twin], acc)
    far, acc = tied((far, acc))
    far_twin = lax.ppermute(far, RING, cross)
    (acc,) = fold(got, [behind_twin, far], acc)
    every = [own, twin, ahead, behind, ahead_twin, behind_twin, far, far_twin]
    unused, out = fold(got, [far_twin], acc, every)

    back = lax.all_to_all(out, ("x", "z"), 0, 0)
    main = back[:, :256, :64].transpose(1, 0, 2).reshape(tokens, SETS * HEAD_DIM)
    level = jnp.sum(back[:, 256:262].astype(F32).reshape(SETS, 3, 256), axis=1).reshape(2, 4, 256)
    share = jnp.exp2(level - jnp.max(level, axis=1, keepdims=True))
    share = share / jnp.sum(share, axis=1, keepdims=True)
    extra = back[:, :256, 64:].astype(F32).reshape(2, 4, 256, HEAD_DIM)
    extra = jnp.sum(extra * share[..., None], axis=1).transpose(1, 0, 2)
    extra = extra.reshape(tokens, 2 * HEAD_DIM)
    attended = jnp.concatenate([main.astype(F32), extra], axis=1)
    return (hidden.astype(F32) + attended).astype(BF16).reshape(rows_here, cols, chans)


def solution(mesh):
    inner = Mesh(mesh.devices.reshape(NX, NZ, NY, NC, -1), BAND + ("img",))
    place = P(("img",) + BAND, None, None)
    in_specs = (place,) + (P(),) * 9
    return jax.shard_map(
        on_device, mesh=inner, in_specs=in_specs, out_specs=place, check_vma=False
    )
```

```python
import functools
import math

import jax
import jax.numpy as jnp
from jax import lax
from jax.experimental import pallas as pl
from jax.experimental.pallas import tpu as pltpu
from jax.sharding import Mesh
from jax.sharding import PartitionSpec as P

HEADS = 10
HEAD_DIM = 64
GROUPS = 16
NX, NZ, NY, NC = (4, 2, 4, 2)
BAND = ("x", "z", "y", "core")
RING = ("y", "core")
SETS = NX * NZ
BANDS = NX * NZ * NY * NC
TILE = 512
TILES = 4
PER_TILE = SETS // TILES
STEPS = 5
LANES = 128
SEND_ROWS = 576
BACK_ROWS = 272
HIGH = 2.0**100
LOW = 2.0**-60
BF16 = jnp.bfloat16
F32 = jnp.float32
VMEM = pltpu.CompilerParams(vmem_limit_bytes=24 * 1024 * 1024)


def total_of(value):
    for axis, size in (("y", NY), (("z", "core"), NZ * NC), ("x", NX)):
        parts = [value]
        for step in range(1, size):
            perm = [(i, (i + step) % size) for i in range(size)]
            parts.append(lax.ppermute(value, axis, perm))
        value = sum(parts[1:], parts[0])
    return value


def halo(latent):
    up = [(i, i + 1) for i in range(BANDS - 1)]
    down = [(j, i) for i, j in up]
    before = lax.ppermute(latent[-1:], BAND, up)
    after = lax.ppermute(latent[:1], BAND, down)
    return before, after


def dot(a, b):
    return jnp.dot(a, b, preferred_element_type=F32)


def swap(a):
    return jnp.concatenate([a[:, 64:128], a[:, 0:64]], axis=1)


def lanes(rows):
    return lax.broadcasted_iota(jnp.int32, (rows, LANES), 1)


def front_kernel(
    sums_ref, vec_ref, before_ref, after_ref, latent_hbm, conv_hbm, wq_hbm, wk_hbm, wv_hbm,
    hidden_ref, send_ref, shift_ref, latent_ref, conv_ref, w_ref, sems,
):
    copies = [pltpu.make_async_copy(latent_hbm, latent_ref, sems.at[0])]
    for i in range(3):
        copies.append(pltpu.make_async_copy(conv_hbm.at[i], conv_ref.at[i], sems.at[1 + i]))
    for i, w_hbm in enumerate((wq_hbm, wk_hbm, wv_hbm)):
        copies.append(pltpu.make_async_copy(w_hbm, w_ref.at[i], sems.at[4 + i]))
    for copy in copies:
        copy.start()
    chans = latent_ref.shape[2]
    count = float(BANDS * 256 * (chans // GROUPS))
    mean = sums_ref[0:1] / count
    var = sums_ref[1:2] / count - mean * mean
    rate = lax.rsqrt(var + 1e-05)
    gain, bias = vec_ref[0:1], vec_ref[1:2]
    row = lax.broadcasted_iota(jnp.int32, (128, chans), 0)
    copies[0].wait()
    sources = [before_ref[0], latent_ref[0], latent_ref[1], after_ref[0]]
    for r, source in enumerate(sources):
        value = (source.astype(F32) - mean) * rate * gain + bias
        act = value / (1.0 + jnp.exp(-value))
        if r == 0:
            act = act * vec_ref[5:6]
        if r == 3:
            act = act * vec_ref[6:7]
        here = slice(128 * r, 128 * r + 128)
        left = jnp.where(row == 0, 0.0, pltpu.roll(act, 1, 0))
        right = jnp.where(row == 127, 0.0, pltpu.roll(act, 127, 0))
        shift_ref[0, here] = left.astype(BF16)
        shift_ref[1, here] = act.astype(BF16)
        shift_ref[2, here] = right.astype(BF16)
    total = latent_ref[...].reshape(256, chans).astype(F32) + vec_ref[2:3]
    for i in range(3):
        copies[1 + i].wait()
        for col in range(3):
            total = total + dot(shift_ref[col, 128 * i : 128 * i + 256, :], conv_ref[i, col])
    hidden = total.astype(BF16)
    hidden_ref[...] = hidden
    values = hidden.astype(F32)
    values = values - jnp.mean(values, axis=1, keepdims=True)
    spread = jnp.mean(values * values, axis=1, keepdims=True)
    normed = (values * lax.rsqrt(spread + 1e-05) * vec_ref[3:4] + vec_ref[4:5]).astype(BF16)
    scale = math.log2(math.e) / math.sqrt(HEAD_DIM)
    copies[4].wait()
    query = (dot(normed, w_ref[0]) * scale).astype(BF16)
    copies[5].wait()
    key = dot(normed, w_ref[1]).T.astype(BF16)
    copies[6].wait()
    value = dot(normed, w_ref[2]).astype(BF16)
    for s in range(SETS):
        main, extra, part = 64 * s, 64 * (SETS + s // 4), 64 * (s % 4)
        send_ref[s, 0:256] = jnp.concatenate(
            [query[:, main : main + 64], query[:, extra : extra + 64]], axis=1
        )
        send_ref[s, 256:320] = key[main : main + 64, 0:128]
        send_ref[s, 320:384] = key[main : main + 64, 128:256]
        send_ref[s, 384:512] = jnp.concatenate(
            [value[0:128, main : main + 64], value[128:256, main : main + 64]], axis=1
        )
        send_ref[s, 512:576] = jnp.concatenate(
            [key[extra : extra + 64, part : part + 64], value[part : part + 64, extra : extra + 64]],
            axis=1,
        )


def front(sums, vec, before, after, latent, conv_weight, w_query, w_key, w_value):
    chans = latent.shape[2]
    far = [latent, conv_weight, w_query, w_key, w_value]
    far = [pltpu.with_memory_space_constraint(a, pltpu.HBM) for a in far]
    return pl.pallas_call(
        front_kernel,
        in_specs=[pl.BlockSpec(memory_space=pltpu.VMEM)] * 4
        + [pl.BlockSpec(memory_space=pltpu.HBM)] * 5,
        out_specs=[pl.BlockSpec(memory_space=pltpu.VMEM)] * 2,
        out_shape=[
            jax.ShapeDtypeStruct((256, chans), BF16),
            jax.ShapeDtypeStruct((SETS, SEND_ROWS, LANES), BF16),
        ],
        scratch_shapes=[
            pltpu.VMEM((3, 512, chans), BF16),
            pltpu.VMEM(latent.shape, BF16),
            pltpu.VMEM(conv_weight.shape, BF16),
            pltpu.VMEM((3, chans, chans), BF16),
            pltpu.SemaphoreType.DMA((7,)),
        ],
        compiler_params=VMEM,
        name="front",
    )(sums, vec, before, after, *far)


def convert_kernel(got_ref, q_ref, kv_ref):
    for src in range(SETS):
        here = slice(256 * src, 256 * src + 256)
        query = got_ref[src, 0:256, :]
        q_ref[0, here] = query
        q_ref[1, here] = swap(query)
        step, odd = src // 2, src % 2
        kv_ref[step, 64 * odd : 64 * odd + 64] = got_ref[src, 256:320, :]
        kv_ref[step, 128 + 64 * odd : 192 + 64 * odd] = got_ref[src, 320:384, :]
        kv_ref[5 + step, 128 * odd : 128 * odd + 128] = got_ref[src, 384:512, :]
    for pair in range(SETS // 2):
        halves = [got_ref[2 * pair + odd, 512:576, 0:64] for odd in range(2)]
        kv_ref[4, 64 * pair : 64 * pair + 64] = jnp.concatenate(halves, axis=1)
        halves = [got_ref[pair + 4 * side, 512:576, 64:128] for side in range(2)]
        kv_ref[9, 64 * pair : 64 * pair + 64] = jnp.concatenate(halves, axis=1)


def near(*arrays):
    return [pltpu.with_memory_space_constraint(a, pltpu.VMEM) for a in arrays]


def convert(got):
    return pl.pallas_call(
        convert_kernel,
        in_specs=[pl.BlockSpec(memory_space=pltpu.VMEM)],
        out_specs=[pl.BlockSpec(memory_space=pltpu.VMEM)] * 2,
        out_shape=[
            pltpu.VMEM((2, TILES * TILE, LANES), BF16),
            pltpu.VMEM((2 * STEPS, 256, LANES), BF16),
        ],
        name="convert",
    )(got)


def step_of(kv_ref, step):
    lane = lanes(256)
    keys = [kv_ref[step, 64 * i : 64 * i + 64, :] for i in range(4)]
    value = kv_ref[STEPS + step]
    values = [jnp.where(lane < 64, side, jnp.ones_like(side)) for side in (value, swap(value))]
    return jnp.concatenate(keys, axis=1), jnp.concatenate(values, axis=0)


def fold_kernel(first, last, q_ref, kv_ref, *refs):
    if not first:
        refs = refs[1:]
    if last:
        far_refs, refs = refs[:SETS], refs[SETS:]
    acc_ref = refs[0]
    tile = pl.program_id(0)
    rows = pl.ds(pl.multiple_of(tile * TILE, TILE), TILE)

    def scores(kind, keys):
        return dot(q_ref[kind, rows, 0:64], keys)

    held = None
    for step in list(range(STEPS)) + [None]:
        if step is not None:
            kind = step // (STEPS - 1)
            keys, values = step_of(kv_ref, step)
            score = scores(kind, keys)
        if held is not None:
            held_step, held_kind, held_score, held_values = held
            update = dot(jnp.exp2(held_score).astype(BF16), held_values)
            if first and held_step in (0, STEPS - 1):
                acc_ref[held_kind, rows] = update
            else:
                acc_ref[held_kind, rows] += update
        held = None if step is None else (step, kind, score, values)

    if last:
        out_ref, store_ref, top_ref, sems = refs[1:]
        lane = lanes(TILE)
        total = jnp.where(lane < 64, swap(acc_ref[1, rows]), acc_ref[0, rows])
        good = (jnp.min(total) > LOW) & (jnp.max(total) < HIGH)
        top_ref[...] = jnp.zeros((2, TILE, LANES), F32)

        @pl.when(jnp.logical_not(good))
        def _():
            copies = []
            for i, far_ref in enumerate(far_refs):
                copies.append(pltpu.make_async_copy(far_ref, store_ref.at[i], sems.at[i]))
                copies[-1].start()
            for kind in range(2):
                acc_ref[kind, rows] = jnp.zeros((TILE, LANES), F32)
            top_ref[...] = jnp.full((2, TILE, LANES), -1e30, F32)
            for copy in copies:
                copy.wait()

            def body(i, carry):
                block, step = i // STEPS, i % STEPS
                kind = step // (STEPS - 1)
                keys, values = step_of(store_ref.at[block], step)
                score = scores(kind, keys)
                top = jnp.maximum(top_ref[kind], jnp.max(score, axis=1, keepdims=True))
                weight = jnp.exp2(score - top[:, 0:1]).astype(BF16)
                factor = jnp.exp2(top_ref[kind] - top)
                acc_ref[kind, rows] = acc_ref[kind, rows] * factor + dot(weight, values)
                top_ref[kind] = top
                return carry

            lax.fori_loop(0, SETS * STEPS, body, 0)

        main, extra = acc_ref[0, rows], acc_ref[1, rows]
        over = swap(extra)
        out = jnp.where(lane < 64, main / swap(main), over / extra).astype(BF16)
        level = (jnp.log2(over) + top_ref[1])[:, 0:1]
        row = lax.broadcasted_iota(jnp.int32, (16, LANES), 0)
        for src in range(PER_TILE):
            out_ref[src, 0:256] = out[256 * src : 256 * src + 256]
            tail = jnp.zeros((16, LANES), F32)
            for half in range(2):
                base = 256 * src + 128 * half
                line = jnp.broadcast_to(level[base : base + 128], (128, LANES)).T[0:16]
                for part in range(3):
                    piece = line.astype(BF16).astype(F32)
                    tail = jnp.where(row == 2 * part + half, piece, tail)
                    line = line - piece
            out_ref[src, 256:272] = tail.astype(BF16)


def fold(query, block, acc, every=None):
    first, last = acc is None, every is not None
    whole = pl.BlockSpec(memory_space=pltpu.VMEM)
    out_specs = [whole]
    out_shape = [pltpu.VMEM(query.shape, F32)]
    scratch = []
    if last:
        out_specs.append(pl.BlockSpec((PER_TILE, BACK_ROWS, LANES), lambda t: (t, 0, 0)))
        out_shape.append(jax.ShapeDtypeStruct((SETS, BACK_ROWS, LANES), BF16))
        scratch = [
            pltpu.VMEM((SETS,) + block.shape, BF16),
            pltpu.VMEM((2, TILE, LANES), F32),
            pltpu.SemaphoreType.DMA((SETS,)),
        ]
    return pl.pallas_call(
        functools.partial(fold_kernel, first, last),
        grid=(TILES,),
        in_specs=[whole] * (2 if first else 3)
        + ([pl.BlockSpec(memory_space=pl.ANY)] * SETS if last else []),
        out_specs=out_specs,
        out_shape=out_shape,
        scratch_shapes=scratch,
        input_output_aliases={} if first else {2: 0},
        compiler_params=VMEM,
        name="fold",
    )(*near(query, block, *(() if first else (acc,))), *(every or ()))


def on_device(
    latent, gn_gain, gn_bias, conv_weight, conv_bias, ln_gain, ln_bias, w_query, w_key, w_value
):
    rows_here, cols, chans = latent.shape
    tokens = rows_here * cols
    width = chans // GROUPS
    before, after = halo(latent)
    flat = latent.astype(F32).reshape(-1, chans)
    sums = jnp.stack([jnp.sum(flat, axis=0), jnp.sum(flat * flat, axis=0)])
    sums = jnp.sum(sums.reshape(2, GROUPS, width), axis=2, keepdims=True)
    sums = total_of(jnp.broadcast_to(sums, (2, GROUPS, width)).reshape(2, chans))
    place = lax.axis_index(BAND)
    row = lax.broadcasted_iota(jnp.int32, (8, chans), 0)
    vec = jnp.where(row == 5, jnp.where(place > 0, 1.0, 0.0), 0.0)
    vec = jnp.where(row == 6, jnp.where(place < BANDS - 1, 1.0, 0.0), vec)
    for i, part in enumerate((gn_gain, gn_bias, conv_bias, ln_gain, ln_bias)):
        vec = jnp.where(row == i, part, vec)
    hidden, send = front(
        sums, vec, before, after, latent, conv_weight, w_query, w_key, w_value
    )

    got = lax.all_to_all(send, ("x", "z"), 0, 0)
    query, own = convert(got)
    spots = [(y, c) for y in range(NY) for c in range(NC)]
    along = [(2 * y + c, 2 * ((y + 1 - 2 * c) % NY) + c) for y, c in spots]
    against = [(j, i) for i, j in along]
    cross = [(2 * y + c, 2 * y + 1 - c) for y, c in spots]

    tied = lax.optimization_barrier
    twin = lax.ppermute(own, RING, cross)
    ahead = lax.ppermute(own, RING, along)
    (acc,) = fold(query, own, None)
    own, acc = tied((own, acc))
    behind = lax.ppermute(own, RING, against)
    (acc,) = fold(query, twin, acc)
    ahead, acc = tied((ahead, acc))
    ahead_twin = lax.ppermute(ahead, RING, cross)
    (acc,) = fold(query, ahead, acc)
    ahead, acc = tied((ahead, acc))
    far = lax.ppermute(ahead, RING, along)
    (acc,) = fold(query, behind, acc)
    behind, acc = tied((behind, acc))
    behind_twin = lax.ppermute(behind, RING, cross)
    (acc,) = fold(query, ahead_twin, acc)
    far, acc = tied((far, acc))
    far_twin = lax.ppermute(far, RING, cross)
    (acc,) = fold(query, behind_twin, acc)
    (acc,) = fold(query, far, acc)
    every = [own, twin, ahead, behind, ahead_twin, behind_twin, far, far_twin]
    unused, out = fold(query, far_twin, acc, every)

    back = lax.all_to_all(out, ("x", "z"), 0, 0)
    main = back[:, :256, :64].transpose(1, 0, 2).reshape(tokens, SETS * HEAD_DIM)
    level = jnp.sum(back[:, 256:262].astype(F32).reshape(SETS, 3, 256), axis=1).reshape(2, 4, 256)
    share = jnp.exp2(level - jnp.max(level, axis=1, keepdims=True))
    share = share / jnp.sum(share, axis=1, keepdims=True)
    extra = back[:, :256, 64:].astype(F32).reshape(2, 4, 256, HEAD_DIM)
    extra = jnp.sum(extra * share[..., None], axis=1).transpose(1, 0, 2)
    extra = extra.reshape(tokens, 2 * HEAD_DIM)
    attended = jnp.concatenate([main.astype(F32), extra], axis=1)
    return (hidden.astype(F32) + attended).astype(BF16).reshape(rows_here, cols, chans)


def solution(mesh):
    inner = Mesh(mesh.devices.reshape(NX, NZ, NY, NC, -1), BAND + ("img",))
    place = P(("img",) + BAND, None, None)
    in_specs = (place,) + (P(),) * 9
    return jax.shard_map(
        on_device, mesh=inner, in_specs=in_specs, out_specs=place, check_vma=False
    )
```

```python
import functools
import math

import jax
import jax.numpy as jnp
from jax import lax
from jax.experimental import pallas as pl
from jax.experimental.pallas import tpu as pltpu
from jax.sharding import Mesh
from jax.sharding import PartitionSpec as P

HEADS = 10
HEAD_DIM = 64
GROUPS = 16
NX, NZ, NY, NC = (4, 2, 4, 2)
BAND = ("x", "z", "y", "core")
RING = ("y", "core")
SETS = NX * NZ
BANDS = NX * NZ * NY * NC
TILE = 512
TILES = 4
LANES = 128
Q_ROWS = 256
KV_ROWS = 320
SEND_ROWS = Q_ROWS + KV_ROWS
BACK_ROWS = 272
HIGH = 2.0**100
LOW = 2.0**-60
BF16 = jnp.bfloat16
F32 = jnp.float32
VMEM = pltpu.CompilerParams(vmem_limit_bytes=24 * 1024 * 1024)


def total_of(value):
    for axis, size in (("y", NY), (("z", "core"), NZ * NC), ("x", NX)):
        parts = [value]
        for step in range(1, size):
            perm = [(i, (i + step) % size) for i in range(size)]
            parts.append(lax.ppermute(value, axis, perm))
        value = sum(parts[1:], parts[0])
    return value


def halo(last, first):
    up = [(i, i + 1) for i in range(BANDS - 1)]
    down = [(j, i) for i, j in up]
    before = lax.ppermute(last, BAND, up)
    after = lax.ppermute(first, BAND, down)
    return before, after


def dot(a, b):
    return jnp.dot(a, b, preferred_element_type=F32)


def swap(a):
    return jnp.concatenate([a[:, 64:128], a[:, 0:64]], axis=1)


def lanes(rows):
    return lax.broadcasted_iota(jnp.int32, (rows, LANES), 1)


def front_kernel(
    sums_ref, vec_ref, before_ref, after_ref, latent_hbm, conv_hbm, wq_hbm, wk_hbm, wv_hbm,
    hidden_ref, send_ref, shift_ref, latent_ref, conv_ref, w_ref, sems,
):
    copies = [pltpu.make_async_copy(latent_hbm, latent_ref, sems.at[0])]
    for i in range(3):
        copies.append(pltpu.make_async_copy(conv_hbm.at[i], conv_ref.at[i], sems.at[1 + i]))
    for i, w_hbm in enumerate((wq_hbm, wk_hbm, wv_hbm)):
        copies.append(pltpu.make_async_copy(w_hbm, w_ref.at[i], sems.at[4 + i]))
    for copy in copies:
        copy.start()
    chans = latent_ref.shape[2]
    count = float(BANDS * 256 * (chans // GROUPS))
    mean = sums_ref[0:1] / count
    var = sums_ref[1:2] / count - mean * mean
    rate = lax.rsqrt(var + 1e-05)
    gain, bias = vec_ref[0:1], vec_ref[1:2]
    row = lax.broadcasted_iota(jnp.int32, (128, chans), 0)
    copies[0].wait()
    sources = [before_ref[0], latent_ref[0], latent_ref[1], after_ref[0]]
    for r, source in enumerate(sources):
        value = (source.astype(F32) - mean) * rate * gain + bias
        act = value / (1.0 + jnp.exp(-value))
        if r == 0:
            act = act * vec_ref[5:6]
        if r == 3:
            act = act * vec_ref[6:7]
        here = slice(128 * r, 128 * r + 128)
        left = jnp.where(row == 0, 0.0, pltpu.roll(act, 1, 0))
        right = jnp.where(row == 127, 0.0, pltpu.roll(act, 127, 0))
        shift_ref[0, here] = left.astype(BF16)
        shift_ref[1, here] = act.astype(BF16)
        shift_ref[2, here] = right.astype(BF16)
    total = latent_ref[...].reshape(256, chans).astype(F32) + vec_ref[2:3]
    for i in range(3):
        copies[1 + i].wait()
        for col in range(3):
            total = total + dot(shift_ref[col, 128 * i : 128 * i + 256, :], conv_ref[i, col])
    hidden = total.astype(BF16)
    hidden_ref[...] = hidden
    values = hidden.astype(F32)
    values = values - jnp.mean(values, axis=1, keepdims=True)
    spread = jnp.mean(values * values, axis=1, keepdims=True)
    normed = (values * lax.rsqrt(spread + 1e-05) * vec_ref[3:4] + vec_ref[4:5]).astype(BF16)
    scale = math.log2(math.e) / math.sqrt(HEAD_DIM)
    copies[4].wait()
    query = (dot(normed, w_ref[0]) * scale).astype(BF16)
    copies[5].wait()
    key = dot(normed, w_ref[1]).T.astype(BF16)
    copies[6].wait()
    value = dot(normed, w_ref[2]).astype(BF16)
    for s in range(SETS):
        main, extra, part = 64 * s, 64 * (SETS + s // 4), 64 * (s % 4)
        send_ref[s, 0:256] = jnp.concatenate(
            [query[:, main : main + 64], query[:, extra : extra + 64]], axis=1
        )
        send_ref[s, 256:320] = key[main : main + 64, 0:128]
        send_ref[s, 320:384] = key[main : main + 64, 128:256]
        send_ref[s, 384:512] = jnp.concatenate(
            [value[0:128, main : main + 64], value[128:256, main : main + 64]], axis=1
        )
        send_ref[s, 512:576] = jnp.concatenate(
            [key[extra : extra + 64, part : part + 64], value[part : part + 64, extra : extra + 64]],
            axis=1,
        )


def front(sums, vec, before, after, latent, conv_weight, w_query, w_key, w_value):
    chans = latent.shape[2]
    far = [latent, conv_weight, w_query, w_key, w_value]
    far = [pltpu.with_memory_space_constraint(a, pltpu.HBM) for a in far]
    return pl.pallas_call(
        front_kernel,
        in_specs=[pl.BlockSpec(memory_space=pltpu.VMEM)] * 4
        + [pl.BlockSpec(memory_space=pltpu.HBM)] * 5,
        out_specs=[pl.BlockSpec(memory_space=pltpu.VMEM)] * 2,
        out_shape=[
            jax.ShapeDtypeStruct((256, chans), BF16),
            jax.ShapeDtypeStruct((SETS, SEND_ROWS, LANES), BF16),
        ],
        scratch_shapes=[
            pltpu.VMEM((3, 512, chans), BF16),
            pltpu.VMEM(latent.shape, BF16),
            pltpu.VMEM(conv_weight.shape, BF16),
            pltpu.VMEM((3, chans, chans), BF16),
            pltpu.SemaphoreType.DMA((7,)),
        ],
        compiler_params=VMEM,
        name="front",
    )(sums, vec, before, after, *far)


def main_step(kv_ref, pair):
    lane = lanes(128)
    keys, values = [], []
    for src in (2 * pair, 2 * pair + 1):
        keys += [kv_ref[src, 0:64, :], kv_ref[src, 64:128, :]]
        value = kv_ref[src, 128:256, :]
        for side in (value, swap(value)):
            values.append(jnp.where(lane < 64, side, jnp.ones_like(side)))
    keys = jnp.concatenate([jnp.concatenate(keys, axis=1), jnp.zeros((64, TILE), BF16)], axis=0)
    return 0, keys, jnp.concatenate(values, axis=0)


def extra_step(kv_ref, block):
    lane = lanes(64)
    sources = [SETS * block + src for src in range(SETS)]
    keys = [kv_ref[src, 256:320, 0:64] for src in sources]
    values = [kv_ref[src, 256:320, :] for src in sources]
    values = [jnp.where(lane >= 64, v, jnp.ones_like(v)) for v in values]
    keys = jnp.concatenate([jnp.zeros((64, TILE), BF16), jnp.concatenate(keys, axis=1)], axis=0)
    return 1, keys, jnp.concatenate(values, axis=0)


def fold_kernel(count, first, last, q_ref, *refs):
    kv_refs, refs = refs[:count], refs[count:]
    if not first:
        acc_in, refs = refs[0], refs[1:]
    if last:
        far_refs, refs = refs[:SETS], refs[SETS:]
    acc_ref = refs[0]
    acc_ref[0] = jnp.zeros((2, TILE, LANES), F32) if first else acc_in[0]
    query = q_ref[...].reshape(TILE, LANES)

    steps = []
    for kv_ref in kv_refs:
        steps += [functools.partial(main_step, kv_ref, pair) for pair in range(SETS // 2)]
        steps.append(functools.partial(extra_step, kv_ref, 0))
    held = None
    for step in steps + [None]:
        if step is not None:
            kind, keys, values = step()
            score = dot(query, keys)
        if held is not None:
            held_kind, held_score, held_values = held
            weight = jnp.exp2(held_score).astype(BF16)
            acc_ref[0, held_kind] += dot(weight, held_values)
        held = None if step is None else (kind, score, values)

    if last:
        out_ref, store_ref, top_ref, sems = refs[1:]
        wide = lanes(TILE)
        total = jnp.where(wide < 64, acc_ref[0, 1], acc_ref[0, 0])
        good = (jnp.min(total) > LOW) & (jnp.max(total) < HIGH)
        top_ref[...] = jnp.zeros((2, TILE, LANES), F32)

        @pl.when(jnp.logical_not(good))
        def _():
            copies = []
            for i, far_ref in enumerate(far_refs):
                here = store_ref.at[pl.ds(SETS * i, SETS)]
                copies.append(pltpu.make_async_copy(far_ref, here, sems.at[i]))
                copies[-1].start()
            acc_ref[0] = jnp.zeros((2, TILE, LANES), F32)
            top_ref[...] = jnp.full((2, TILE, LANES), -1e30, F32)
            for copy in copies:
                copy.wait()

            def online(step):
                kind, keys, values = step
                score = dot(query, keys)
                top = jnp.maximum(top_ref[kind], jnp.max(score, axis=1, keepdims=True))
                weight = jnp.exp2(score - top[:, 0:1]).astype(BF16)
                factor = jnp.exp2(top_ref[kind] - top)
                acc_ref[0, kind] = acc_ref[0, kind] * factor + dot(weight, values)
                top_ref[kind] = top

            def pair_body(pair, carry):
                online(main_step(store_ref, pair))
                return carry

            def block_body(block, carry):
                online(extra_step(store_ref, block))
                return carry

            lax.fori_loop(0, SETS * SETS // 2, pair_body, 0)
            lax.fori_loop(0, SETS, block_body, 0)

        main, extra = acc_ref[0, 0], acc_ref[0, 1]
        out = jnp.where(wide < 64, main, extra) / jnp.where(wide < 64, swap(main), swap(extra))
        out = out.astype(BF16)
        level = (jnp.log2(extra) + top_ref[1])[:, 0:1]
        row = lax.broadcasted_iota(jnp.int32, (16, LANES), 0)
        for src in range(2):
            out_ref[src, 0:256] = out[256 * src : 256 * src + 256]
            tail = jnp.zeros((16, LANES), F32)
            for half in range(2):
                base = 256 * src + 128 * half
                line = jnp.broadcast_to(level[base : base + 128], (128, LANES)).T[0:16]
                for part in range(3):
                    piece = line.astype(BF16).astype(F32)
                    tail = jnp.where(row == 2 * part + half, piece, tail)
                    line = line - piece
            out_ref[src, 256:272] = tail.astype(BF16)


def fold(got, blocks, acc, every=None):
    first, last = acc is None, every is not None
    acc_spec = pl.BlockSpec((1, 2, TILE, LANES), lambda t: (t, 0, 0, 0))
    kv_spec = pl.BlockSpec((SETS, KV_ROWS, LANES), lambda t: (0, 0, 0))
    out_specs = [acc_spec]
    out_shape = [jax.ShapeDtypeStruct((TILES, 2, TILE, LANES), F32)]
    scratch = []
    if last:
        out_specs.append(pl.BlockSpec((2, BACK_ROWS, LANES), lambda t: (t, 0, 0)))
        out_shape.append(jax.ShapeDtypeStruct((SETS, BACK_ROWS, LANES), BF16))
        scratch = [
            pltpu.VMEM((SETS * SETS, KV_ROWS, LANES), BF16),
            pltpu.VMEM((2, TILE, LANES), F32),
            pltpu.SemaphoreType.DMA((SETS,)),
        ]
    return pl.pallas_call(
        functools.partial(fold_kernel, len(blocks), first, last),
        grid=(TILES,),
        in_specs=[pl.BlockSpec((2, Q_ROWS, LANES), lambda t: (t, 0, 0))]
        + [kv_spec] * len(blocks)
        + ([] if first else [acc_spec])
        + ([pl.BlockSpec(memory_space=pl.ANY)] * SETS if last else []),
        out_specs=out_specs,
        out_shape=out_shape,
        scratch_shapes=scratch,
        input_output_aliases={} if first else {1 + len(blocks): 0},
        compiler_params=VMEM,
        name="fold",
    )(got, *blocks, *(() if first else (acc,)), *(every or ()))


def on_device(
    latent, gn_gain, gn_bias, conv_weight, conv_bias, ln_gain, ln_bias, w_query, w_key, w_value
):
    rows_here, cols, chans = latent.shape
    tokens = rows_here * cols
    width = chans // GROUPS
    edges = lax.optimization_barrier((latent[-1:], latent[:1], latent))
    before, after = halo(*edges[:2])
    flat = edges[2].astype(F32).reshape(-1, chans)
    sums = jnp.stack([jnp.sum(flat, axis=0), jnp.sum(flat * flat, axis=0)])
    sums = jnp.sum(sums.reshape(2, GROUPS, width), axis=2, keepdims=True)
    sums = total_of(jnp.broadcast_to(sums, (2, GROUPS, width)).reshape(2, chans))
    place = lax.axis_index(BAND)
    row = lax.broadcasted_iota(jnp.int32, (8, chans), 0)
    vec = jnp.where(row == 5, jnp.where(place > 0, 1.0, 0.0), 0.0)
    vec = jnp.where(row == 6, jnp.where(place < BANDS - 1, 1.0, 0.0), vec)
    for i, part in enumerate((gn_gain, gn_bias, conv_bias, ln_gain, ln_bias)):
        vec = jnp.where(row == i, part, vec)
    hidden, send = front(
        sums, vec, before, after, latent, conv_weight, w_query, w_key, w_value
    )

    got = lax.all_to_all(send, ("x", "z"), 0, 0)
    own = got[:, Q_ROWS:]
    spots = [(y, c) for y in range(NY) for c in range(NC)]
    along = [(2 * y + c, 2 * ((y + 1 - 2 * c) % NY) + c) for y, c in spots]
    against = [(j, i) for i, j in along]
    cross = [(2 * y + c, 2 * y + 1 - c) for y, c in spots]

    tied = lax.optimization_barrier
    twin = lax.ppermute(own, RING, cross)
    ahead = lax.ppermute(own, RING, along)
    (acc,) = fold(got, [own], None)
    own, acc = tied((own, acc))
    behind = lax.ppermute(own, RING, against)
    (acc,) = fold(got, [twin], acc)
    ahead, acc = tied((ahead, acc))
    ahead_twin = lax.ppermute(ahead, RING, cross)
    (acc,) = fold(got, [ahead], acc)
    ahead, acc = tied((ahead, acc))
    far = lax.ppermute(ahead, RING, along)
    (acc,) = fold(got, [behind], acc)
    behind, acc = tied((behind, acc))
    behind_twin = lax.ppermute(behind, RING, cross)
    (acc,) = fold(got, [ahead_twin], acc)
    far, acc = tied((far, acc))
    far_twin = lax.ppermute(far, RING, cross)
    (acc,) = fold(got, [behind_twin, far], acc)
    every = [own, twin, ahead, behind, ahead_twin, behind_twin, far, far_twin]
    unused, out = fold(got, [far_twin], acc, every)

    back = lax.all_to_all(out, ("x", "z"), 0, 0)
    main = back[:, :256, :64].transpose(1, 0, 2).reshape(tokens, SETS * HEAD_DIM)
    level = jnp.sum(back[:, 256:262].astype(F32).reshape(SETS, 3, 256), axis=1).reshape(2, 4, 256)
    share = jnp.exp2(level - jnp.max(level, axis=1, keepdims=True))
    share = share / jnp.sum(share, axis=1, keepdims=True)
    extra = back[:, :256, 64:].astype(F32).reshape(2, 4, 256, HEAD_DIM)
    extra = jnp.sum(extra * share[..., None], axis=1).transpose(1, 0, 2)
    extra = extra.reshape(tokens, 2 * HEAD_DIM)
    attended = jnp.concatenate([main.astype(F32), extra], axis=1)
    return (hidden.astype(F32) + attended).astype(BF16).reshape(rows_here, cols, chans)


def solution(mesh):
    inner = Mesh(mesh.devices.reshape(NX, NZ, NY, NC, -1), BAND + ("img",))
    place = P(("img",) + BAND, None, None)
    in_specs = (place,) + (P(),) * 9
    return jax.shard_map(
        on_device, mesh=inner, in_specs=in_specs, out_specs=place, check_vma=False
    )
```

```python
import functools
import math

import jax
import jax.numpy as jnp
from jax import lax
from jax.experimental import pallas as pl
from jax.experimental.pallas import tpu as pltpu
from jax.sharding import Mesh
from jax.sharding import PartitionSpec as P

HEADS = 10
HEAD_DIM = 64
GROUPS = 16
NX, NZ, NY, NC = (4, 2, 4, 2)
BAND = ("x", "z", "y", "core")
RING = ("y", "core")
SETS = NX * NZ
BANDS = NX * NZ * NY * NC
SPAN = 512
TOKENS = 2048
LANES = 128
Q_ROWS = 256
KV_ROWS = 320
SEND_ROWS = Q_ROWS + KV_ROWS
BACK_ROWS = 272
HIGH = 2.0**100
LOW = 2.0**-60
BF16 = jnp.bfloat16
F32 = jnp.float32
VMEM = pltpu.CompilerParams(vmem_limit_bytes=24 * 1024 * 1024)


def total_of(value):
    for axis, size in (("y", NY), (("z", "core"), NZ * NC), ("x", NX)):
        parts = [value]
        for step in range(1, size):
            perm = [(i, (i + step) % size) for i in range(size)]
            parts.append(lax.ppermute(value, axis, perm))
        value = sum(parts[1:], parts[0])
    return value


def halo(last, first):
    up = [(i, i + 1) for i in range(BANDS - 1)]
    down = [(j, i) for i, j in up]
    before = lax.ppermute(last, BAND, up)
    after = lax.ppermute(first, BAND, down)
    return before, after


def dot(a, b):
    return jnp.dot(a, b, preferred_element_type=F32)


def swap(a):
    return jnp.concatenate([a[:, 64:128], a[:, 0:64]], axis=1)


def lanes(rows):
    return lax.broadcasted_iota(jnp.int32, (rows, LANES), 1)


def begin_kernel(latent_hbm, sums_ref, last_ref, first_ref, latent_ref, sem):
    copy = pltpu.make_async_copy(latent_hbm, latent_ref, sem.at[0])
    copy.start()
    copy.wait()
    first, last = latent_ref[0].astype(F32), latent_ref[1].astype(F32)
    sums_ref[0:1] = jnp.sum(first + last, axis=0, keepdims=True)
    sums_ref[1:2] = jnp.sum(first * first + last * last, axis=0, keepdims=True)
    last_ref[0] = latent_ref[1]
    first_ref[0] = latent_ref[0]


def begin(latent):
    edge = jax.ShapeDtypeStruct((1,) + latent.shape[1:], BF16)
    return pl.pallas_call(
        begin_kernel,
        in_specs=[pl.BlockSpec(memory_space=pltpu.HBM)],
        out_specs=[pl.BlockSpec(memory_space=pltpu.VMEM)] * 3,
        out_shape=[jax.ShapeDtypeStruct((2, latent.shape[2]), F32), edge, edge],
        scratch_shapes=[pltpu.VMEM(latent.shape, BF16), pltpu.SemaphoreType.DMA((1,))],
        name="begin",
    )(pltpu.with_memory_space_constraint(latent, pltpu.HBM))


def front_kernel(
    sums_ref, vec_ref, before_ref, after_ref, latent_hbm, conv_hbm, wq_hbm, wk_hbm, wv_hbm,
    hidden_ref, send_ref, shift_ref, latent_ref, conv_ref, w_ref, sems,
):
    copies = [pltpu.make_async_copy(latent_hbm, latent_ref, sems.at[0])]
    for i in range(3):
        copies.append(pltpu.make_async_copy(conv_hbm.at[i], conv_ref.at[i], sems.at[1 + i]))
    for i, w_hbm in enumerate((wq_hbm, wk_hbm, wv_hbm)):
        copies.append(pltpu.make_async_copy(w_hbm, w_ref.at[i], sems.at[4 + i]))
    for copy in copies:
        copy.start()
    chans = latent_ref.shape[2]
    count = float(BANDS * 256 * (chans // GROUPS))
    mean = sums_ref[0:1] / count
    var = sums_ref[1:2] / count - mean * mean
    rate = lax.rsqrt(var + 1e-05)
    gain, bias, conv_bias, ln_gain, ln_bias = [vec_ref[i : i + 1] for i in range(5)]
    row = lax.broadcasted_iota(jnp.int32, (128, chans), 0)
    copies[0].wait()
    sources = [before_ref[0], latent_ref[0], latent_ref[1], after_ref[0]]
    for r, source in enumerate(sources):
        value = (source.astype(F32) - mean) * rate * gain + bias
        act = value / (1.0 + jnp.exp(-value))
        if r == 0:
            act = act * vec_ref[5:6]
        if r == 3:
            act = act * vec_ref[6:7]
        here = slice(128 * r, 128 * r + 128)
        left = jnp.where(row == 0, 0.0, pltpu.roll(act, 1, 0))
        right = jnp.where(row == 127, 0.0, pltpu.roll(act, 127, 0))
        shift_ref[0, here] = left.astype(BF16)
        shift_ref[1, here] = act.astype(BF16)
        shift_ref[2, here] = right.astype(BF16)
    total = latent_ref[...].reshape(256, chans).astype(F32) + conv_bias
    for i in range(3):
        copies[1 + i].wait()
        for col in range(3):
            total = total + dot(shift_ref[col, 128 * i : 128 * i + 256, :], conv_ref[i, col])
    hidden = total.astype(BF16)
    hidden_ref[...] = hidden
    values = hidden.astype(F32)
    values = values - jnp.mean(values, axis=1, keepdims=True)
    spread = jnp.mean(values * values, axis=1, keepdims=True)
    normed = (values * lax.rsqrt(spread + 1e-05) * ln_gain + ln_bias).astype(BF16)
    scale = math.log2(math.e) / math.sqrt(HEAD_DIM)
    copies[4].wait()
    query = (dot(normed, w_ref[0]) * scale).astype(BF16)
    copies[5].wait()
    key = dot(normed, w_ref[1]).T.astype(BF16)
    copies[6].wait()
    value = dot(normed, w_ref[2]).astype(BF16)
    for s in range(SETS):
        main, extra, part = 64 * s, 64 * (SETS + s // 4), 64 * (s % 4)
        send_ref[s, 0:256] = jnp.concatenate(
            [query[:, main : main + 64], query[:, extra : extra + 64]], axis=1
        )
        send_ref[s, 256:320] = key[main : main + 64, 0:128]
        send_ref[s, 320:384] = key[main : main + 64, 128:256]
        send_ref[s, 384:512] = jnp.concatenate(
            [value[0:128, main : main + 64], value[128:256, main : main + 64]], axis=1
        )
        send_ref[s, 512:576] = jnp.concatenate(
            [key[extra : extra + 64, part : part + 64], value[part : part + 64, extra : extra + 64]],
            axis=1,
        )


def front(sums, vec, before, after, latent, conv_weight, w_query, w_key, w_value):
    chans = latent.shape[2]
    far = [latent, conv_weight, w_query, w_key, w_value]
    far = [pltpu.with_memory_space_constraint(a, pltpu.HBM) for a in far]
    return pl.pallas_call(
        front_kernel,
        in_specs=[pl.BlockSpec(memory_space=pltpu.VMEM)] * 4
        + [pl.BlockSpec(memory_space=pltpu.HBM)] * 5,
        out_specs=[pl.BlockSpec(memory_space=pltpu.VMEM)] * 2,
        out_shape=[
            jax.ShapeDtypeStruct((256, chans), BF16),
            jax.ShapeDtypeStruct((SETS, SEND_ROWS, LANES), BF16),
        ],
        scratch_shapes=[
            pltpu.VMEM((3, 512, chans), BF16),
            pltpu.VMEM(latent.shape, BF16),
            pltpu.VMEM(conv_weight.shape, BF16),
            pltpu.VMEM((3, chans, chans), BF16),
            pltpu.SemaphoreType.DMA((7,)),
        ],
        compiler_params=VMEM,
        name="front",
    )(sums, vec, before, after, *far)


def main_step(kv_ref, pair):
    lane = lanes(128)
    keys, values = [], []
    for src in (2 * pair, 2 * pair + 1):
        keys += [kv_ref[src, 0:64, :], kv_ref[src, 64:128, :]]
        value = kv_ref[src, 128:256, :]
        for side in (value, swap(value)):
            values.append(jnp.where(lane < 64, side, jnp.ones_like(side)))
    keys = jnp.concatenate([jnp.concatenate(keys, axis=1), jnp.zeros((64, SPAN), BF16)], axis=0)
    return 0, keys, jnp.concatenate(values, axis=0)


def extra_step(kv_ref, block):
    lane = lanes(64)
    sources = [SETS * block + src for src in range(SETS)]
    keys = [kv_ref[src, 256:320, 0:64] for src in sources]
    values = [kv_ref[src, 256:320, :] for src in sources]
    values = [jnp.where(lane >= 64, v, jnp.ones_like(v)) for v in values]
    keys = jnp.concatenate([jnp.zeros((64, SPAN), BF16), jnp.concatenate(keys, axis=1)], axis=0)
    return 1, keys, jnp.concatenate(values, axis=0)


def fold_kernel(count, tile, first, last, q_ref, *refs):
    kv_refs, refs = refs[:count], refs[count:]
    if not first:
        acc_in, refs = refs[0], refs[1:]
    if last:
        far_refs, refs = refs[:SETS], refs[SETS:]
    acc_ref = refs[0]
    acc_ref[...] = jnp.zeros((2, tile, LANES), F32) if first else acc_in[...]
    query = q_ref[...].reshape(tile, LANES)

    steps = []
    for kv_ref in kv_refs:
        steps += [functools.partial(main_step, kv_ref, pair) for pair in range(SETS // 2)]
        steps.append(functools.partial(extra_step, kv_ref, 0))
    held = None
    for step in steps + [None]:
        if step is not None:
            kind, keys, values = step()
            score = dot(query, keys)
        if held is not None:
            held_kind, held_score, held_values = held
            weight = jnp.exp2(held_score).astype(BF16)
            acc_ref[held_kind] += dot(weight, held_values)
        held = None if step is None else (kind, score, values)

    if last:
        out_ref, store_ref, top_ref, sems = refs[1:]
        wide = lanes(tile)
        total = jnp.where(wide < 64, acc_ref[1], acc_ref[0])
        good = (jnp.min(total) > LOW) & (jnp.max(total) < HIGH)
        top_ref[...] = jnp.zeros((2, tile, LANES), F32)

        @pl.when(jnp.logical_not(good))
        def _():
            copies = []
            for i, far_ref in enumerate(far_refs):
                here = store_ref.at[pl.ds(SETS * i, SETS)]
                copies.append(pltpu.make_async_copy(far_ref, here, sems.at[i]))
                copies[-1].start()
            acc_ref[...] = jnp.zeros((2, tile, LANES), F32)
            top_ref[...] = jnp.full((2, tile, LANES), -1e30, F32)
            for copy in copies:
                copy.wait()

            def online(step):
                kind, keys, values = step
                score = dot(query, keys)
                top = jnp.maximum(top_ref[kind], jnp.max(score, axis=1, keepdims=True))
                weight = jnp.exp2(score - top[:, 0:1]).astype(BF16)
                factor = jnp.exp2(top_ref[kind] - top)
                acc_ref[kind] = acc_ref[kind] * factor + dot(weight, values)
                top_ref[kind] = top

            def pair_body(pair, carry):
                online(main_step(store_ref, pair))
                return carry

            def block_body(block, carry):
                online(extra_step(store_ref, block))
                return carry

            lax.fori_loop(0, SETS * SETS // 2, pair_body, 0)
            lax.fori_loop(0, SETS, block_body, 0)

        main, extra = acc_ref[0], acc_ref[1]
        out = jnp.where(wide < 64, main, extra) / jnp.where(wide < 64, swap(main), swap(extra))
        out = out.astype(BF16)
        level = (jnp.log2(extra) + top_ref[1])[:, 0:1]
        row = lax.broadcasted_iota(jnp.int32, (16, LANES), 0)
        for src in range(tile // 256):
            out_ref[src, 0:256] = out[256 * src : 256 * src + 256]
            tail = jnp.zeros((16, LANES), F32)
            for half in range(2):
                base = 256 * src + 128 * half
                line = jnp.broadcast_to(level[base : base + 128], (128, LANES)).T[0:16]
                for part in range(3):
                    piece = line.astype(BF16).astype(F32)
                    tail = jnp.where(row == 2 * part + half, piece, tail)
                    line = line - piece
            out_ref[src, 256:272] = tail.astype(BF16)


def fold(got, blocks, acc, every=None, tile=512):
    first, last = acc is None, every is not None
    acc_spec = pl.BlockSpec((2, tile, LANES), lambda t: (0, t, 0))
    kv_spec = pl.BlockSpec((SETS, KV_ROWS, LANES), lambda t: (0, 0, 0))
    out_specs = [acc_spec]
    out_shape = [jax.ShapeDtypeStruct((2, TOKENS, LANES), F32)]
    scratch = []
    if last:
        out_specs.append(pl.BlockSpec((tile // 256, BACK_ROWS, LANES), lambda t: (t, 0, 0)))
        out_shape.append(jax.ShapeDtypeStruct((SETS, BACK_ROWS, LANES), BF16))
        scratch = [
            pltpu.VMEM((SETS * SETS, KV_ROWS, LANES), BF16),
            pltpu.VMEM((2, tile, LANES), F32),
            pltpu.SemaphoreType.DMA((SETS,)),
        ]
    return pl.pallas_call(
        functools.partial(fold_kernel, len(blocks), tile, first, last),
        grid=(TOKENS // tile,),
        in_specs=[pl.BlockSpec((tile // 256, Q_ROWS, LANES), lambda t: (t, 0, 0))]
        + [kv_spec] * len(blocks)
        + ([] if first else [acc_spec])
        + ([pl.BlockSpec(memory_space=pl.ANY)] * SETS if last else []),
        out_specs=out_specs,
        out_shape=out_shape,
        scratch_shapes=scratch,
        input_output_aliases={} if first else {1 + len(blocks): 0},
        compiler_params=VMEM,
        name="fold",
    )(got, *blocks, *(() if first else (acc,)), *(every or ()))


def finish_kernel(back_ref, hidden_ref, out_ref):
    for pair in range(SETS // 2):
        here = slice(128 * pair, 128 * pair + 128)
        both = [back_ref[2 * pair, 0:256, 0:64], back_ref[2 * pair + 1, 0:256, 0:64]]
        both = jnp.concatenate(both, axis=1).astype(F32)
        out_ref[:, here] = (hidden_ref[:, here].astype(F32) + both).astype(BF16)
    for half in range(2):
        rows = slice(128 * half, 128 * half + 128)
        shares = []
        for head in range(2):
            levels = []
            for s in range(4 * head, 4 * head + 4):
                tail = back_ref[s, 256:272].astype(F32)
                levels.append(sum(tail[2 * p + half : 2 * p + half + 1] for p in range(3)))
            top = functools.reduce(jnp.maximum, levels)
            parts = [jnp.exp2(level - top) for level in levels]
            total = sum(parts)
            shares += [part / total for part in parts]
        table = jnp.concatenate(shares + [jnp.zeros((LANES - SETS, LANES), F32)], axis=0).T
        both = []
        for head in range(2):
            value = jnp.zeros((128, 64), F32)
            for s in range(4 * head, 4 * head + 4):
                part = back_ref[s, rows, 64:128].astype(F32)
                value = value + part * jnp.broadcast_to(table[:, s : s + 1], (128, 64))
            both.append(value)
        here = slice(64 * SETS, 64 * SETS + 128)
        value = hidden_ref[rows, here].astype(F32) + jnp.concatenate(both, axis=1)
        out_ref[rows, here] = value.astype(BF16)


def finish(back, hidden):
    return pl.pallas_call(
        finish_kernel,
        in_specs=[pl.BlockSpec(memory_space=pltpu.VMEM)] * 2,
        out_specs=pl.BlockSpec(memory_space=pltpu.VMEM),
        out_shape=jax.ShapeDtypeStruct(hidden.shape, BF16),
        name="finish",
    )(*[pltpu.with_memory_space_constraint(a, pltpu.VMEM) for a in (back, hidden)])


def on_device(
    latent, gn_gain, gn_bias, conv_weight, conv_bias, ln_gain, ln_bias, w_query, w_key, w_value
):
    rows_here, cols, chans = latent.shape
    width = chans // GROUPS
    sums, last, first = begin(latent)
    before, after = halo(last, first)
    sums = total_of(sums)
    sums = jnp.sum(sums.reshape(2, GROUPS, width), axis=2, keepdims=True)
    sums = jnp.broadcast_to(sums, (2, GROUPS, width)).reshape(2, chans)
    place = lax.axis_index(BAND)
    row = lax.broadcasted_iota(jnp.int32, (8, chans), 0)
    vec = jnp.where(row == 5, jnp.where(place > 0, 1.0, 0.0), 0.0)
    vec = jnp.where(row == 6, jnp.where(place < BANDS - 1, 1.0, 0.0), vec)
    for i, part in enumerate((gn_gain, gn_bias, conv_bias, ln_gain, ln_bias)):
        vec = jnp.where(row == i, part, vec)
    hidden, send = front(
        sums, vec, before, after, latent, conv_weight, w_query, w_key, w_value
    )

    got = lax.all_to_all(send, ("x", "z"), 0, 0)
    own = got[:, Q_ROWS:]
    spots = [(y, c) for y in range(NY) for c in range(NC)]
    along = [(2 * y + c, 2 * ((y + 1 - 2 * c) % NY) + c) for y, c in spots]
    against = [(j, i) for i, j in along]
    cross = [(2 * y + c, 2 * y + 1 - c) for y, c in spots]

    tied = lax.optimization_barrier
    twin = lax.ppermute(own, RING, cross)
    ahead = lax.ppermute(own, RING, along)
    (acc,) = fold(got, [own], None)
    own, acc = tied((own, acc))
    behind = lax.ppermute(own, RING, against)
    (acc,) = fold(got, [twin], acc)
    ahead, acc = tied((ahead, acc))
    ahead_twin = lax.ppermute(ahead, RING, cross)
    (acc,) = fold(got, [ahead], acc, tile=1024)
    ahead, acc = tied((ahead, acc))
    far = lax.ppermute(ahead, RING, along)
    (acc,) = fold(got, [behind], acc, tile=1024)
    behind, acc = tied((behind, acc))
    behind_twin = lax.ppermute(behind, RING, cross)
    (acc,) = fold(got, [ahead_twin], acc)
    far, acc = tied((far, acc))
    far_twin = lax.ppermute(far, RING, cross)
    (acc,) = fold(got, [behind_twin, far], acc)
    every = [own, twin, ahead, behind, ahead_twin, behind_twin, far, far_twin]
    unused, out = fold(got, [far_twin], acc, every)

    back = lax.all_to_all(out, ("x", "z"), 0, 0)
    return finish(back, hidden).reshape(rows_here, cols, chans)


def solution(mesh):
    inner = Mesh(mesh.devices.reshape(NX, NZ, NY, NC, -1), BAND + ("img",))
    place = P(("img",) + BAND, None, None)
    in_specs = (place,) + (P(),) * 9
    return jax.shard_map(
        on_device, mesh=inner, in_specs=in_specs, out_specs=place, check_vma=False
    )
```

```python
import functools
import math

import jax
import jax.numpy as jnp
from jax import lax
from jax.experimental import pallas as pl
from jax.experimental.pallas import tpu as pltpu
from jax.sharding import Mesh
from jax.sharding import PartitionSpec as P

HEADS = 10
HEAD_DIM = 64
GROUPS = 16
NX, NZ, NY, NC = (4, 2, 4, 2)
BAND = ("x", "z", "y", "core")
RING = ("y", "core")
SETS = NX * NZ
BANDS = NX * NZ * NY * NC
SPAN = 512
TOKENS = 2048
LANES = 128
Q_ROWS = 256
KV_ROWS = 320
SEND_ROWS = Q_ROWS + KV_ROWS
BACK_ROWS = 272
HIGH = 2.0**100
LOW = 2.0**-60
BF16 = jnp.bfloat16
F32 = jnp.float32
VMEM = pltpu.CompilerParams(vmem_limit_bytes=24 * 1024 * 1024)


def total_of(value):
    for axis, size in (("y", NY), (("z", "core"), NZ * NC), ("x", NX)):
        parts = [value]
        for step in range(1, size):
            perm = [(i, (i + step) % size) for i in range(size)]
            parts.append(lax.ppermute(value, axis, perm))
        value = sum(parts[1:], parts[0])
    return value


def halo(last, first):
    up = [(i, i + 1) for i in range(BANDS - 1)]
    down = [(j, i) for i, j in up]
    before = lax.ppermute(last, BAND, up)
    after = lax.ppermute(first, BAND, down)
    return before, after


def dot(a, b):
    return jnp.dot(a, b, preferred_element_type=F32)


def swap(a):
    return jnp.concatenate([a[:, 64:128], a[:, 0:64]], axis=1)


def lanes(rows):
    return lax.broadcasted_iota(jnp.int32, (rows, LANES), 1)


def begin_kernel(
    latent_hbm, wq_hbm, wk_hbm, wv_hbm, sums_ref, last_ref, first_ref, w_ref, latent_ref, sems
):
    copies = [pltpu.make_async_copy(latent_hbm, latent_ref, sems.at[0])]
    for i, w_hbm in enumerate((wq_hbm, wk_hbm, wv_hbm)):
        copies.append(pltpu.make_async_copy(w_hbm, w_ref.at[i], sems.at[1 + i]))
    for copy in copies:
        copy.start()
    copies[0].wait()
    first, last = latent_ref[0].astype(F32), latent_ref[1].astype(F32)
    sums_ref[0:1] = jnp.sum(first + last, axis=0, keepdims=True)
    sums_ref[1:2] = jnp.sum(first * first + last * last, axis=0, keepdims=True)
    last_ref[0] = latent_ref[1]
    first_ref[0] = latent_ref[0]
    for copy in copies[1:]:
        copy.wait()


def begin(latent, w_query, w_key, w_value):
    edge = jax.ShapeDtypeStruct((1,) + latent.shape[1:], BF16)
    far = [latent, w_query, w_key, w_value]
    far = [pltpu.with_memory_space_constraint(a, pltpu.HBM) for a in far]
    return pl.pallas_call(
        begin_kernel,
        in_specs=[pl.BlockSpec(memory_space=pltpu.HBM)] * 4,
        out_specs=[pl.BlockSpec(memory_space=pltpu.VMEM)] * 4,
        out_shape=[
            pltpu.VMEM((2, latent.shape[2]), F32),
            edge,
            edge,
            pltpu.VMEM((3,) + w_query.shape, BF16),
        ],
        scratch_shapes=[pltpu.VMEM(latent.shape, BF16), pltpu.SemaphoreType.DMA((4,))],
        name="begin",
    )(*far)


def front_kernel(
    sums_ref, vec_ref, before_ref, after_ref, w_ref, latent_hbm, conv_hbm,
    hidden_ref, send_ref, shift_ref, latent_ref, conv_ref, sems,
):
    copies = [pltpu.make_async_copy(latent_hbm, latent_ref, sems.at[0])]
    for i in range(3):
        copies.append(pltpu.make_async_copy(conv_hbm.at[i], conv_ref.at[i], sems.at[1 + i]))
    for copy in copies:
        copy.start()
    chans = latent_ref.shape[2]
    count = float(BANDS * 256 * (chans // GROUPS))
    mean = sums_ref[0:1] / count
    var = sums_ref[1:2] / count - mean * mean
    rate = lax.rsqrt(var + 1e-05)
    gain, bias, conv_bias, ln_gain, ln_bias = [vec_ref[i : i + 1] for i in range(5)]
    row = lax.broadcasted_iota(jnp.int32, (128, chans), 0)
    copies[0].wait()
    sources = [before_ref[0], latent_ref[0], latent_ref[1], after_ref[0]]
    for r, source in enumerate(sources):
        value = (source.astype(F32) - mean) * rate * gain + bias
        act = value / (1.0 + jnp.exp(-value))
        if r == 0:
            act = act * vec_ref[5:6]
        if r == 3:
            act = act * vec_ref[6:7]
        here = slice(128 * r, 128 * r + 128)
        left = jnp.where(row == 0, 0.0, pltpu.roll(act, 1, 0))
        right = jnp.where(row == 127, 0.0, pltpu.roll(act, 127, 0))
        shift_ref[0, here] = left.astype(BF16)
        shift_ref[1, here] = act.astype(BF16)
        shift_ref[2, here] = right.astype(BF16)
    total = latent_ref[...].reshape(256, chans).astype(F32) + conv_bias
    for i in range(3):
        copies[1 + i].wait()
        for col in range(3):
            total = total + dot(shift_ref[col, 128 * i : 128 * i + 256, :], conv_ref[i, col])
    hidden = total.astype(BF16)
    hidden_ref[...] = hidden
    values = hidden.astype(F32)
    values = values - jnp.mean(values, axis=1, keepdims=True)
    spread = jnp.mean(values * values, axis=1, keepdims=True)
    normed = (values * lax.rsqrt(spread + 1e-05) * ln_gain + ln_bias).astype(BF16)
    scale = math.log2(math.e) / math.sqrt(HEAD_DIM)
    query = (dot(normed, w_ref[0]) * scale).astype(BF16)
    key = dot(normed, w_ref[1]).T.astype(BF16)
    value = dot(normed, w_ref[2]).astype(BF16)
    for s in range(SETS):
        main, extra, part = 64 * s, 64 * (SETS + s // 4), 64 * (s % 4)
        send_ref[s, 0:256] = jnp.concatenate(
            [query[:, main : main + 64], query[:, extra : extra + 64]], axis=1
        )
        send_ref[s, 256:320] = key[main : main + 64, 0:128]
        send_ref[s, 320:384] = key[main : main + 64, 128:256]
        send_ref[s, 384:512] = jnp.concatenate(
            [value[0:128, main : main + 64], value[128:256, main : main + 64]], axis=1
        )
        send_ref[s, 512:576] = jnp.concatenate(
            [key[extra : extra + 64, part : part + 64], value[part : part + 64, extra : extra + 64]],
            axis=1,
        )


def front(sums, vec, before, after, weights, latent, conv_weight):
    chans = latent.shape[2]
    far = [pltpu.with_memory_space_constraint(a, pltpu.HBM) for a in (latent, conv_weight)]
    near = pltpu.with_memory_space_constraint(weights, pltpu.VMEM)
    return pl.pallas_call(
        front_kernel,
        in_specs=[pl.BlockSpec(memory_space=pltpu.VMEM)] * 5
        + [pl.BlockSpec(memory_space=pltpu.HBM)] * 2,
        out_specs=[pl.BlockSpec(memory_space=pltpu.VMEM)] * 2,
        out_shape=[
            jax.ShapeDtypeStruct((256, chans), BF16),
            jax.ShapeDtypeStruct((SETS, SEND_ROWS, LANES), BF16),
        ],
        scratch_shapes=[
            pltpu.VMEM((3, 512, chans), BF16),
            pltpu.VMEM(latent.shape, BF16),
            pltpu.VMEM(conv_weight.shape, BF16),
            pltpu.SemaphoreType.DMA((4,)),
        ],
        compiler_params=VMEM,
        name="front",
    )(sums, vec, before, after, near, *far)


def main_step(kv_ref, pair):
    lane = lanes(128)
    keys, values = [], []
    for src in (2 * pair, 2 * pair + 1):
        keys += [kv_ref[src, 0:64, :], kv_ref[src, 64:128, :]]
        value = kv_ref[src, 128:256, :]
        for side in (value, swap(value)):
            values.append(jnp.where(lane < 64, side, jnp.ones_like(side)))
    keys = jnp.concatenate([jnp.concatenate(keys, axis=1), jnp.zeros((64, SPAN), BF16)], axis=0)
    return 0, keys, jnp.concatenate(values, axis=0)


def extra_step(kv_ref, block):
    lane = lanes(64)
    sources = [SETS * block + src for src in range(SETS)]
    keys = [kv_ref[src, 256:320, 0:64] for src in sources]
    values = [kv_ref[src, 256:320, :] for src in sources]
    values = [jnp.where(lane >= 64, v, jnp.ones_like(v)) for v in values]
    keys = jnp.concatenate([jnp.zeros((64, SPAN), BF16), jnp.concatenate(keys, axis=1)], axis=0)
    return 1, keys, jnp.concatenate(values, axis=0)


def fold_kernel(count, tile, first, last, q_ref, *refs):
    kv_refs, refs = refs[:count], refs[count:]
    if not first:
        acc_in, refs = refs[0], refs[1:]
    if last:
        far_refs, refs = refs[:SETS], refs[SETS:]
    acc_ref = refs[0]
    acc_ref[...] = jnp.zeros(acc_ref.shape, F32) if first else acc_in[...]
    query = q_ref[...].reshape(tile, LANES)

    steps = []
    for kv_ref in kv_refs:
        steps += [functools.partial(main_step, kv_ref, pair) for pair in range(SETS // 2)]
        steps.append(functools.partial(extra_step, kv_ref, 0))
    held = None
    for step in steps + [None]:
        if step is not None:
            kind, keys, values = step()
            score = dot(query, keys)
        if held is not None:
            held_kind, held_score, held_values = held
            weight = jnp.exp2(held_score).astype(BF16)
            update = dot(weight, held_values)
            for i in range(tile // SPAN):
                acc_ref[i, held_kind] += update[SPAN * i : SPAN * i + SPAN]
        held = None if step is None else (kind, score, values)

    if last:
        out_ref, store_ref, top_ref, sems = refs[1:]
        wide = lanes(tile)
        total = jnp.where(wide < 64, acc_ref[0, 1], acc_ref[0, 0])
        good = (jnp.min(total) > LOW) & (jnp.max(total) < HIGH)
        top_ref[...] = jnp.zeros((2, tile, LANES), F32)

        @pl.when(jnp.logical_not(good))
        def _():
            copies = []
            for i, far_ref in enumerate(far_refs):
                here = store_ref.at[pl.ds(SETS * i, SETS)]
                copies.append(pltpu.make_async_copy(far_ref, here, sems.at[i]))
                copies[-1].start()
            acc_ref[...] = jnp.zeros(acc_ref.shape, F32)
            top_ref[...] = jnp.full((2, tile, LANES), -1e30, F32)
            for copy in copies:
                copy.wait()

            def online(step):
                kind, keys, values = step
                score = dot(query, keys)
                top = jnp.maximum(top_ref[kind], jnp.max(score, axis=1, keepdims=True))
                weight = jnp.exp2(score - top[:, 0:1]).astype(BF16)
                factor = jnp.exp2(top_ref[kind] - top)
                acc_ref[0, kind] = acc_ref[0, kind] * factor + dot(weight, values)
                top_ref[kind] = top

            def pair_body(pair, carry):
                online(main_step(store_ref, pair))
                return carry

            def block_body(block, carry):
                online(extra_step(store_ref, block))
                return carry

            lax.fori_loop(0, SETS * SETS // 2, pair_body, 0)
            lax.fori_loop(0, SETS, block_body, 0)

        main, extra = acc_ref[0, 0], acc_ref[0, 1]
        out = jnp.where(wide < 64, main, extra) / jnp.where(wide < 64, swap(main), swap(extra))
        out = out.astype(BF16)
        level = (jnp.log2(extra) + top_ref[1])[:, 0:1]
        row = lax.broadcasted_iota(jnp.int32, (16, LANES), 0)
        for src in range(tile // 256):
            out_ref[src, 0:256] = out[256 * src : 256 * src + 256]
            tail = jnp.zeros((16, LANES), F32)
            for half in range(2):
                base = 256 * src + 128 * half
                line = jnp.broadcast_to(level[base : base + 128], (128, LANES)).T[0:16]
                for part in range(3):
                    piece = line.astype(BF16).astype(F32)
                    tail = jnp.where(row == 2 * part + half, piece, tail)
                    line = line - piece
            out_ref[src, 256:272] = tail.astype(BF16)


def fold(got, blocks, acc, every=None, tile=SPAN):
    first, last = acc is None, every is not None
    acc_spec = pl.BlockSpec((tile // SPAN, 2, SPAN, LANES), lambda t: (t, 0, 0, 0))
    kv_spec = pl.BlockSpec((SETS, KV_ROWS, LANES), lambda t: (0, 0, 0))
    out_specs = [acc_spec]
    out_shape = [jax.ShapeDtypeStruct((TOKENS // SPAN, 2, SPAN, LANES), F32)]
    scratch = []
    if last:
        out_specs.append(pl.BlockSpec((tile // 256, BACK_ROWS, LANES), lambda t: (t, 0, 0)))
        out_shape.append(jax.ShapeDtypeStruct((SETS, BACK_ROWS, LANES), BF16))
        scratch = [
            pltpu.VMEM((SETS * SETS, KV_ROWS, LANES), BF16),
            pltpu.VMEM((2, tile, LANES), F32),
            pltpu.SemaphoreType.DMA((SETS,)),
        ]
    return pl.pallas_call(
        functools.partial(fold_kernel, len(blocks), tile, first, last),
        grid=(TOKENS // tile,),
        in_specs=[pl.BlockSpec((tile // 256, Q_ROWS, LANES), lambda t: (t, 0, 0))]
        + [kv_spec] * len(blocks)
        + ([] if first else [acc_spec])
        + ([pl.BlockSpec(memory_space=pl.ANY)] * SETS if last else []),
        out_specs=out_specs,
        out_shape=out_shape,
        scratch_shapes=scratch,
        input_output_aliases={} if first else {1 + len(blocks): 0},
        compiler_params=VMEM,
        name="fold",
    )(got, *blocks, *(() if first else (acc,)), *(every or ()))


def finish_kernel(back_ref, hidden_ref, out_ref):
    for pair in range(SETS // 2):
        here = slice(128 * pair, 128 * pair + 128)
        both = [back_ref[2 * pair, 0:256, 0:64], back_ref[2 * pair + 1, 0:256, 0:64]]
        both = jnp.concatenate(both, axis=1).astype(F32)
        out_ref[:, here] = (hidden_ref[:, here].astype(F32) + both).astype(BF16)
    for half in range(2):
        rows = slice(128 * half, 128 * half + 128)
        shares = []
        for head in range(2):
            levels = []
            for s in range(4 * head, 4 * head + 4):
                tail = back_ref[s, 256:272].astype(F32)
                levels.append(sum(tail[2 * p + half : 2 * p + half + 1] for p in range(3)))
            top = functools.reduce(jnp.maximum, levels)
            parts = [jnp.exp2(level - top) for level in levels]
            total = sum(parts)
            shares += [part / total for part in parts]
        table = jnp.concatenate(shares + [jnp.zeros((LANES - SETS, LANES), F32)], axis=0).T
        both = []
        for head in range(2):
            value = jnp.zeros((128, 64), F32)
            for s in range(4 * head, 4 * head + 4):
                part = back_ref[s, rows, 64:128].astype(F32)
                value = value + part * jnp.broadcast_to(table[:, s : s + 1], (128, 64))
            both.append(value)
        here = slice(64 * SETS, 64 * SETS + 128)
        value = hidden_ref[rows, here].astype(F32) + jnp.concatenate(both, axis=1)
        out_ref[rows, here] = value.astype(BF16)


def finish(back, hidden):
    return pl.pallas_call(
        finish_kernel,
        in_specs=[pl.BlockSpec(memory_space=pltpu.VMEM)] * 2,
        out_specs=pl.BlockSpec(memory_space=pltpu.VMEM),
        out_shape=jax.ShapeDtypeStruct(hidden.shape, BF16),
        name="finish",
    )(*[pltpu.with_memory_space_constraint(a, pltpu.VMEM) for a in (back, hidden)])


def on_device(
    latent, gn_gain, gn_bias, conv_weight, conv_bias, ln_gain, ln_bias, w_query, w_key, w_value
):
    rows_here, cols, chans = latent.shape
    width = chans // GROUPS
    sums, last, first, weights = begin(latent, w_query, w_key, w_value)
    before, after = halo(last, first)
    sums = total_of(sums)
    sums = jnp.sum(sums.reshape(2, GROUPS, width), axis=2, keepdims=True)
    sums = jnp.broadcast_to(sums, (2, GROUPS, width)).reshape(2, chans)
    place = lax.axis_index(BAND)
    row = lax.broadcasted_iota(jnp.int32, (8, chans), 0)
    vec = jnp.where(row == 5, jnp.where(place > 0, 1.0, 0.0), 0.0)
    vec = jnp.where(row == 6, jnp.where(place < BANDS - 1, 1.0, 0.0), vec)
    for i, part in enumerate((gn_gain, gn_bias, conv_bias, ln_gain, ln_bias)):
        vec = jnp.where(row == i, part, vec)
    hidden, send = front(sums, vec, before, after, weights, latent, conv_weight)

    got = lax.all_to_all(send, ("x", "z"), 0, 0)
    own = got[:, Q_ROWS:]
    spots = [(y, c) for y in range(NY) for c in range(NC)]
    along = [(2 * y + c, 2 * ((y + 1 - 2 * c) % NY) + c) for y, c in spots]
    against = [(j, i) for i, j in along]
    cross = [(2 * y + c, 2 * y + 1 - c) for y, c in spots]

    tied = lax.optimization_barrier
    twin = lax.ppermute(own, RING, cross)
    ahead = lax.ppermute(own, RING, along)
    (acc,) = fold(got, [own], None)
    own, acc = tied((own, acc))
    behind = lax.ppermute(own, RING, against)
    (acc,) = fold(got, [twin], acc)
    ahead, acc = tied((ahead, acc))
    ahead_twin = lax.ppermute(ahead, RING, cross)
    (acc,) = fold(got, [ahead], acc, tile=1024)
    ahead, acc = tied((ahead, acc))
    far = lax.ppermute(ahead, RING, along)
    (acc,) = fold(got, [behind], acc, tile=1024)
    behind, acc = tied((behind, acc))
    behind_twin = lax.ppermute(behind, RING, cross)
    (acc,) = fold(got, [ahead_twin], acc)
    far, acc = tied((far, acc))
    far_twin = lax.ppermute(far, RING, cross)
    (acc,) = fold(got, [behind_twin, far], acc)
    every = [own, twin, ahead, behind, ahead_twin, behind_twin, far, far_twin]
    unused, out = fold(got, [far_twin], acc, every)

    back = lax.all_to_all(out, ("x", "z"), 0, 0)
    return finish(back, hidden).reshape(rows_here, cols, chans)


def solution(mesh):
    inner = Mesh(mesh.devices.reshape(NX, NZ, NY, NC, -1), BAND + ("img",))
    place = P(("img",) + BAND, None, None)
    in_specs = (place,) + (P(),) * 9
    return jax.shard_map(
        on_device, mesh=inner, in_specs=in_specs, out_specs=place, check_vma=False
    )
```

```python
import functools
import math

import jax
import jax.numpy as jnp
from jax import lax
from jax.experimental import pallas as pl
from jax.experimental.pallas import tpu as pltpu
from jax.sharding import Mesh
from jax.sharding import PartitionSpec as P

HEADS = 10
HEAD_DIM = 64
GROUPS = 16
NX, NZ, NY, NC = (4, 2, 4, 2)
BAND = ("x", "z", "y", "core")
RING = ("y", "core")
SETS = NX * NZ
BANDS = NX * NZ * NY * NC
SPAN = 512
TOKENS = 2048
ACC = 1024
LANES = 128
Q_ROWS = 256
KV_ROWS = 320
SEND_ROWS = Q_ROWS + KV_ROWS
BACK_ROWS = 272
HIGH = 2.0**100
LOW = 2.0**-60
BF16 = jnp.bfloat16
F32 = jnp.float32
VMEM = pltpu.CompilerParams(vmem_limit_bytes=24 * 1024 * 1024)


def total_of(value):
    for axis, size in (("y", NY), (("z", "core"), NZ * NC), ("x", NX)):
        parts = [value]
        for step in range(1, size):
            perm = [(i, (i + step) % size) for i in range(size)]
            parts.append(lax.ppermute(value, axis, perm))
        value = sum(parts[1:], parts[0])
    return value


def halo(last, first):
    up = [(i, i + 1) for i in range(BANDS - 1)]
    down = [(j, i) for i, j in up]
    before = lax.ppermute(last, BAND, up)
    after = lax.ppermute(first, BAND, down)
    return before, after


def dot(a, b):
    return jnp.dot(a, b, preferred_element_type=F32)


def swap(a):
    return jnp.concatenate([a[:, 64:128], a[:, 0:64]], axis=1)


def lanes(rows):
    return lax.broadcasted_iota(jnp.int32, (rows, LANES), 1)


def begin_kernel(latent_hbm, sums_ref, last_ref, first_ref, latent_ref, sem):
    copy = pltpu.make_async_copy(latent_hbm, latent_ref, sem.at[0])
    copy.start()
    copy.wait()
    first, last = latent_ref[0].astype(F32), latent_ref[1].astype(F32)
    sums_ref[0:1] = jnp.sum(first + last, axis=0, keepdims=True)
    sums_ref[1:2] = jnp.sum(first * first + last * last, axis=0, keepdims=True)
    last_ref[0] = latent_ref[1]
    first_ref[0] = latent_ref[0]


def begin(latent):
    edge = jax.ShapeDtypeStruct((1,) + latent.shape[1:], BF16)
    return pl.pallas_call(
        begin_kernel,
        in_specs=[pl.BlockSpec(memory_space=pltpu.HBM)],
        out_specs=[pl.BlockSpec(memory_space=pltpu.VMEM)] * 3,
        out_shape=[pltpu.VMEM((2, latent.shape[2]), F32), edge, edge],
        scratch_shapes=[pltpu.VMEM(latent.shape, BF16), pltpu.SemaphoreType.DMA((1,))],
        name="begin",
    )(pltpu.with_memory_space_constraint(latent, pltpu.HBM))


def front_kernel(
    sums_ref, vec_ref, before_ref, after_ref, latent_hbm, conv_hbm, wq_hbm, wk_hbm, wv_hbm,
    hidden_ref, send_ref, shift_ref, latent_ref, conv_ref, w_ref, sems,
):
    copies = [pltpu.make_async_copy(latent_hbm, latent_ref, sems.at[0])]
    for i in range(3):
        copies.append(pltpu.make_async_copy(conv_hbm.at[i], conv_ref.at[i], sems.at[1 + i]))
    for i, w_hbm in enumerate((wq_hbm, wk_hbm, wv_hbm)):
        copies.append(pltpu.make_async_copy(w_hbm, w_ref.at[i], sems.at[4 + i]))
    for copy in copies:
        copy.start()
    chans = latent_ref.shape[2]
    count = float(BANDS * 256 * (chans // GROUPS))
    mean = sums_ref[0:1] / count
    var = sums_ref[1:2] / count - mean * mean
    rate = lax.rsqrt(var + 1e-05)
    gain, bias, conv_bias, ln_gain, ln_bias = [vec_ref[i : i + 1] for i in range(5)]
    row = lax.broadcasted_iota(jnp.int32, (128, chans), 0)
    copies[0].wait()
    sources = [before_ref[0], latent_ref[0], latent_ref[1], after_ref[0]]
    for r, source in enumerate(sources):
        value = (source.astype(F32) - mean) * rate * gain + bias
        act = value / (1.0 + jnp.exp(-value))
        if r == 0:
            act = act * vec_ref[5:6]
        if r == 3:
            act = act * vec_ref[6:7]
        here = slice(128 * r, 128 * r + 128)
        left = jnp.where(row == 0, 0.0, pltpu.roll(act, 1, 0))
        right = jnp.where(row == 127, 0.0, pltpu.roll(act, 127, 0))
        shift_ref[0, here] = left.astype(BF16)
        shift_ref[1, here] = act.astype(BF16)
        shift_ref[2, here] = right.astype(BF16)
    total = latent_ref[...].reshape(256, chans).astype(F32) + conv_bias
    for i in range(3):
        copies[1 + i].wait()
        for col in range(3):
            total = total + dot(shift_ref[col, 128 * i : 128 * i + 256, :], conv_ref[i, col])
    hidden = total.astype(BF16)
    hidden_ref[...] = hidden
    values = hidden.astype(F32)
    values = values - jnp.mean(values, axis=1, keepdims=True)
    spread = jnp.mean(values * values, axis=1, keepdims=True)
    normed = (values * lax.rsqrt(spread + 1e-05) * ln_gain + ln_bias).astype(BF16)
    scale = math.log2(math.e) / math.sqrt(HEAD_DIM)
    copies[4].wait()
    query = (dot(normed, w_ref[0]) * scale).astype(BF16)
    copies[5].wait()
    key = dot(normed, w_ref[1]).T.astype(BF16)
    copies[6].wait()
    value = dot(normed, w_ref[2]).astype(BF16)
    for s in range(SETS):
        main, extra, part = 64 * s, 64 * (SETS + s // 4), 64 * (s % 4)
        send_ref[s, 0:256] = jnp.concatenate(
            [query[:, main : main + 64], query[:, extra : extra + 64]], axis=1
        )
        send_ref[s, 256:320] = key[main : main + 64, 0:128]
        send_ref[s, 320:384] = key[main : main + 64, 128:256]
        send_ref[s, 384:512] = jnp.concatenate(
            [value[0:128, main : main + 64], value[128:256, main : main + 64]], axis=1
        )
        send_ref[s, 512:576] = jnp.concatenate(
            [key[extra : extra + 64, part : part + 64], value[part : part + 64, extra : extra + 64]],
            axis=1,
        )


def front(sums, vec, before, after, latent, conv_weight, w_query, w_key, w_value):
    chans = latent.shape[2]
    far = [latent, conv_weight, w_query, w_key, w_value]
    far = [pltpu.with_memory_space_constraint(a, pltpu.HBM) for a in far]
    return pl.pallas_call(
        front_kernel,
        in_specs=[pl.BlockSpec(memory_space=pltpu.VMEM)] * 4
        + [pl.BlockSpec(memory_space=pltpu.HBM)] * 5,
        out_specs=[pl.BlockSpec(memory_space=pltpu.VMEM)] * 2,
        out_shape=[
            jax.ShapeDtypeStruct((256, chans), BF16),
            jax.ShapeDtypeStruct((SETS, SEND_ROWS, LANES), BF16),
        ],
        scratch_shapes=[
            pltpu.VMEM((3, 512, chans), BF16),
            pltpu.VMEM(latent.shape, BF16),
            pltpu.VMEM(conv_weight.shape, BF16),
            pltpu.VMEM((3, chans, chans), BF16),
            pltpu.SemaphoreType.DMA((7,)),
        ],
        compiler_params=VMEM,
        name="front",
    )(sums, vec, before, after, *far)


def main_step(kv_ref, pair):
    lane = lanes(128)
    keys, values = [], []
    for src in (2 * pair, 2 * pair + 1):
        keys += [kv_ref[src, 0:64, :], kv_ref[src, 64:128, :]]
        value = kv_ref[src, 128:256, :]
        for side in (value, swap(value)):
            values.append(jnp.where(lane < 64, side, jnp.ones_like(side)))
    keys = jnp.concatenate([jnp.concatenate(keys, axis=1), jnp.zeros((64, SPAN), BF16)], axis=0)
    return 0, keys, jnp.concatenate(values, axis=0)


def extra_step(kv_ref, block):
    lane = lanes(64)
    sources = [SETS * block + src for src in range(SETS)]
    keys = [kv_ref[src, 256:320, 0:64] for src in sources]
    values = [kv_ref[src, 256:320, :] for src in sources]
    values = [jnp.where(lane >= 64, v, jnp.ones_like(v)) for v in values]
    keys = jnp.concatenate([jnp.zeros((64, SPAN), BF16), jnp.concatenate(keys, axis=1)], axis=0)
    return 1, keys, jnp.concatenate(values, axis=0)


def fold_kernel(count, tile, first, last, q_ref, *refs):
    block = pl.program_id(1)
    kv_refs, refs = refs[:count], refs[count:]
    if not first:
        acc_in, refs = refs[0], refs[1:]
    if last:
        far_refs, refs = refs[:SETS], refs[SETS:]
    acc_ref = refs[0]
    if count == 1:
        kv_ref = kv_refs[0]
    else:
        kv_ref = refs[-1]
        for i in range(count):

            @pl.when(block == i)
            def _():
                kv_ref[...] = kv_refs[i][...]

    @pl.when(block == 0)
    def _():
        acc_ref[...] = jnp.zeros(acc_ref.shape, F32) if first else acc_in[...]

    query = q_ref[...].reshape(tile, LANES)

    steps = [functools.partial(main_step, kv_ref, pair) for pair in range(SETS // 2)]
    steps.append(functools.partial(extra_step, kv_ref, 0))
    held = None
    for step in steps + [None]:
        if step is not None:
            kind, keys, values = step()
            score = dot(query, keys)
        if held is not None:
            held_kind, held_score, held_values = held
            weight = jnp.exp2(held_score).astype(BF16)
            acc_ref[0, held_kind] += dot(weight, held_values)
        held = None if step is None else (kind, score, values)

    if last:
        out_ref, store_ref, top_ref, sems = refs[1:]
        wide = lanes(tile)
        total = jnp.where(wide < 64, acc_ref[0, 1], acc_ref[0, 0])
        good = (jnp.min(total) > LOW) & (jnp.max(total) < HIGH)
        top_ref[...] = jnp.zeros((2, tile, LANES), F32)

        @pl.when(jnp.logical_not(good))
        def _():
            copies = []
            for i, far_ref in enumerate(far_refs):
                here = store_ref.at[pl.ds(SETS * i, SETS)]
                copies.append(pltpu.make_async_copy(far_ref, here, sems.at[i]))
                copies[-1].start()
            acc_ref[...] = jnp.zeros(acc_ref.shape, F32)
            top_ref[...] = jnp.full((2, tile, LANES), -1e30, F32)
            for copy in copies:
                copy.wait()

            def online(step):
                kind, keys, values = step
                score = dot(query, keys)
                top = jnp.maximum(top_ref[kind], jnp.max(score, axis=1, keepdims=True))
                weight = jnp.exp2(score - top[:, 0:1]).astype(BF16)
                factor = jnp.exp2(top_ref[kind] - top)
                acc_ref[0, kind] = acc_ref[0, kind] * factor + dot(weight, values)
                top_ref[kind] = top

            def pair_body(pair, carry):
                online(main_step(store_ref, pair))
                return carry

            def block_body(block, carry):
                online(extra_step(store_ref, block))
                return carry

            lax.fori_loop(0, SETS * SETS // 2, pair_body, 0)
            lax.fori_loop(0, SETS, block_body, 0)

        main, extra = acc_ref[0, 0], acc_ref[0, 1]
        out = jnp.where(wide < 64, main, extra) / jnp.where(wide < 64, swap(main), swap(extra))
        out = out.astype(BF16)
        level = (jnp.log2(extra) + top_ref[1])[:, 0:1]
        row = lax.broadcasted_iota(jnp.int32, (16, LANES), 0)
        for src in range(tile // 256):
            out_ref[src, 0:256] = out[256 * src : 256 * src + 256]
            tail = jnp.zeros((16, LANES), F32)
            for half in range(2):
                base = 256 * src + 128 * half
                line = jnp.broadcast_to(level[base : base + 128], (128, LANES)).T[0:16]
                for part in range(3):
                    piece = line.astype(BF16).astype(F32)
                    tail = jnp.where(row == 2 * part + half, piece, tail)
                    line = line - piece
            out_ref[src, 256:272] = tail.astype(BF16)


def fold(got, blocks, acc, every=None, tile=512):
    per = ACC // tile
    first, last = acc is None, every is not None
    acc_spec = pl.BlockSpec((1, 2, tile, LANES), lambda t, b: (t // per, 0, t % per, 0))
    kv_spec = pl.BlockSpec((SETS, KV_ROWS, LANES), lambda t, b: (0, 0, 0))
    out_specs = [acc_spec]
    out_shape = [jax.ShapeDtypeStruct((TOKENS // ACC, 2, ACC, LANES), F32)]
    scratch = [pltpu.VMEM(blocks[0].shape, BF16)] if len(blocks) > 1 else []
    if last:
        out_specs.append(pl.BlockSpec((tile // 256, BACK_ROWS, LANES), lambda t, b: (t, 0, 0)))
        out_shape.append(jax.ShapeDtypeStruct((SETS, BACK_ROWS, LANES), BF16))
        scratch = [
            pltpu.VMEM((SETS * SETS, KV_ROWS, LANES), BF16),
            pltpu.VMEM((2, tile, LANES), F32),
            pltpu.SemaphoreType.DMA((SETS,)),
        ]
    return pl.pallas_call(
        functools.partial(fold_kernel, len(blocks), tile, first, last),
        grid=(TOKENS // tile, len(blocks)),
        in_specs=[pl.BlockSpec((tile // 256, Q_ROWS, LANES), lambda t, b: (t, 0, 0))]
        + [kv_spec] * len(blocks)
        + ([] if first else [acc_spec])
        + ([pl.BlockSpec(memory_space=pl.ANY)] * SETS if last else []),
        out_specs=out_specs,
        out_shape=out_shape,
        scratch_shapes=scratch,
        input_output_aliases={} if first else {1 + len(blocks): 0},
        compiler_params=VMEM,
        name="fold",
    )(got, *blocks, *(() if first else (acc,)), *(every or ()))


def finish_kernel(back_ref, hidden_ref, out_ref):
    for pair in range(SETS // 2):
        here = slice(128 * pair, 128 * pair + 128)
        both = [back_ref[2 * pair, 0:256, 0:64], back_ref[2 * pair + 1, 0:256, 0:64]]
        both = jnp.concatenate(both, axis=1).astype(F32)
        out_ref[:, here] = (hidden_ref[:, here].astype(F32) + both).astype(BF16)
    for half in range(2):
        rows = slice(128 * half, 128 * half + 128)
        shares = []
        for head in range(2):
            levels = []
            for s in range(4 * head, 4 * head + 4):
                tail = back_ref[s, 256:272].astype(F32)
                levels.append(sum(tail[2 * p + half : 2 * p + half + 1] for p in range(3)))
            top = functools.reduce(jnp.maximum, levels)
            parts = [jnp.exp2(level - top) for level in levels]
            total = sum(parts)
            shares += [part / total for part in parts]
        table = jnp.concatenate(shares + [jnp.zeros((LANES - SETS, LANES), F32)], axis=0).T
        both = []
        for head in range(2):
            value = jnp.zeros((128, 64), F32)
            for s in range(4 * head, 4 * head + 4):
                part = back_ref[s, rows, 64:128].astype(F32)
                value = value + part * jnp.broadcast_to(table[:, s : s + 1], (128, 64))
            both.append(value)
        here = slice(64 * SETS, 64 * SETS + 128)
        value = hidden_ref[rows, here].astype(F32) + jnp.concatenate(both, axis=1)
        out_ref[rows, here] = value.astype(BF16)


def finish(back, hidden):
    return pl.pallas_call(
        finish_kernel,
        in_specs=[pl.BlockSpec(memory_space=pltpu.VMEM)] * 2,
        out_specs=pl.BlockSpec(memory_space=pltpu.VMEM),
        out_shape=jax.ShapeDtypeStruct(hidden.shape, BF16),
        name="finish",
    )(*[pltpu.with_memory_space_constraint(a, pltpu.VMEM) for a in (back, hidden)])


def on_device(
    latent, gn_gain, gn_bias, conv_weight, conv_bias, ln_gain, ln_bias, w_query, w_key, w_value
):
    rows_here, cols, chans = latent.shape
    width = chans // GROUPS
    sums, last, first = begin(latent)
    before, after = halo(last, first)
    sums = total_of(sums)
    sums = jnp.sum(sums.reshape(2, GROUPS, width), axis=2, keepdims=True)
    sums = jnp.broadcast_to(sums, (2, GROUPS, width)).reshape(2, chans)
    place = lax.axis_index(BAND)
    row = lax.broadcasted_iota(jnp.int32, (8, chans), 0)
    vec = jnp.where(row == 5, jnp.where(place > 0, 1.0, 0.0), 0.0)
    vec = jnp.where(row == 6, jnp.where(place < BANDS - 1, 1.0, 0.0), vec)
    for i, part in enumerate((gn_gain, gn_bias, conv_bias, ln_gain, ln_bias)):
        vec = jnp.where(row == i, part, vec)
    hidden, send = front(
        sums, vec, before, after, latent, conv_weight, w_query, w_key, w_value
    )

    got = lax.all_to_all(send, ("x", "z"), 0, 0)
    own = got[:, Q_ROWS:]
    spots = [(y, c) for y in range(NY) for c in range(NC)]
    along = [(2 * y + c, 2 * ((y + 1 - 2 * c) % NY) + c) for y, c in spots]
    against = [(j, i) for i, j in along]
    cross = [(2 * y + c, 2 * y + 1 - c) for y, c in spots]

    tied = lax.optimization_barrier
    twin = lax.ppermute(own, RING, cross)
    ahead = lax.ppermute(own, RING, along)
    (acc,) = fold(got, [own], None)
    own, acc = tied((own, acc))
    behind = lax.ppermute(own, RING, against)
    (acc,) = fold(got, [twin], acc)
    ahead, acc = tied((ahead, acc))
    ahead_twin = lax.ppermute(ahead, RING, cross)
    (acc,) = fold(got, [ahead], acc)
    ahead, acc = tied((ahead, acc))
    far = lax.ppermute(ahead, RING, along)
    (acc,) = fold(got, [behind], acc, tile=1024)
    behind, acc = tied((behind, acc))
    behind_twin = lax.ppermute(behind, RING, cross)
    (acc,) = fold(got, [ahead_twin], acc, tile=1024)
    far, acc = tied((far, acc))
    far_twin = lax.ppermute(far, RING, cross)
    (acc,) = fold(got, [behind_twin, far], acc, tile=1024)
    every = [own, twin, ahead, behind, ahead_twin, behind_twin, far, far_twin]
    unused, out = fold(got, [far_twin], acc, every)

    back = lax.all_to_all(out, ("x", "z"), 0, 0)
    return finish(back, hidden).reshape(rows_here, cols, chans)


def solution(mesh):
    inner = Mesh(mesh.devices.reshape(NX, NZ, NY, NC, -1), BAND + ("img",))
    place = P(("img",) + BAND, None, None)
    in_specs = (place,) + (P(),) * 9
    return jax.shard_map(
        on_device, mesh=inner, in_specs=in_specs, out_specs=place, check_vma=False
    )
```

```python
import functools
import math

import jax
import jax.numpy as jnp
from jax import lax
from jax.experimental import pallas as pl
from jax.experimental.pallas import tpu as pltpu
from jax.sharding import Mesh
from jax.sharding import PartitionSpec as P

HEADS = 10
HEAD_DIM = 64
GROUPS = 16
NX, NZ, NY, NC = (4, 2, 4, 2)
BAND = ("x", "z", "y", "core")
RING = ("y", "core")
SETS = NX * NZ
BANDS = NX * NZ * NY * NC
SPAN = 512
TOKENS = 2048
ACC = 1024
LANES = 128
Q_ROWS = 256
KV_ROWS = 320
SEND_ROWS = Q_ROWS + KV_ROWS
BACK_ROWS = 272
HIGH = 2.0**100
LOW = 2.0**-60
BF16 = jnp.bfloat16
F32 = jnp.float32
VMEM = pltpu.CompilerParams(vmem_limit_bytes=24 * 1024 * 1024)


def total_of(value):
    for axis, size in (("y", NY), (("z", "core"), NZ * NC), ("x", NX)):
        parts = [value]
        for step in range(1, size):
            perm = [(i, (i + step) % size) for i in range(size)]
            parts.append(lax.ppermute(value, axis, perm))
        value = sum(parts[1:], parts[0])
    return value


def halo(last, first):
    up = [(i, i + 1) for i in range(BANDS - 1)]
    down = [(j, i) for i, j in up]
    before = lax.ppermute(last, BAND, up)
    after = lax.ppermute(first, BAND, down)
    return before, after


def dot(a, b):
    return jnp.dot(a, b, preferred_element_type=F32)


def swap(a):
    return jnp.concatenate([a[:, 64:128], a[:, 0:64]], axis=1)


def lanes(rows):
    return lax.broadcasted_iota(jnp.int32, (rows, LANES), 1)


def begin_kernel(latent_hbm, sums_ref, last_ref, first_ref, latent_ref, sem):
    copy = pltpu.make_async_copy(latent_hbm, latent_ref, sem.at[0])
    copy.start()
    copy.wait()
    first, last = latent_ref[0].astype(F32), latent_ref[1].astype(F32)
    sums_ref[0:1] = jnp.sum(first + last, axis=0, keepdims=True)
    sums_ref[1:2] = jnp.sum(first * first + last * last, axis=0, keepdims=True)
    last_ref[0] = latent_ref[1]
    first_ref[0] = latent_ref[0]


def begin(latent):
    edge = jax.ShapeDtypeStruct((1,) + latent.shape[1:], BF16)
    return pl.pallas_call(
        begin_kernel,
        in_specs=[pl.BlockSpec(memory_space=pltpu.HBM)],
        out_specs=[pl.BlockSpec(memory_space=pltpu.VMEM)] * 3,
        out_shape=[pltpu.VMEM((2, latent.shape[2]), F32), edge, edge],
        scratch_shapes=[pltpu.VMEM(latent.shape, BF16), pltpu.SemaphoreType.DMA((1,))],
        name="begin",
    )(pltpu.with_memory_space_constraint(latent, pltpu.HBM))


def front_kernel(
    sums_ref, vec_ref, before_ref, after_ref, latent_hbm, conv_hbm, wq_hbm, wk_hbm, wv_hbm,
    hidden_ref, send_ref, shift_ref, latent_ref, conv_ref, w_ref, sems,
):
    copies = [pltpu.make_async_copy(latent_hbm, latent_ref, sems.at[0])]
    for i in range(3):
        copies.append(pltpu.make_async_copy(conv_hbm.at[i], conv_ref.at[i], sems.at[1 + i]))
    for i, w_hbm in enumerate((wq_hbm, wk_hbm, wv_hbm)):
        copies.append(pltpu.make_async_copy(w_hbm, w_ref.at[i], sems.at[4 + i]))
    for copy in copies:
        copy.start()
    chans = latent_ref.shape[2]
    count = float(BANDS * 256 * (chans // GROUPS))
    mean = sums_ref[0:1] / count
    var = sums_ref[1:2] / count - mean * mean
    rate = lax.rsqrt(var + 1e-05)
    gain, bias, conv_bias, ln_gain, ln_bias = [vec_ref[i : i + 1] for i in range(5)]
    row = lax.broadcasted_iota(jnp.int32, (128, chans), 0)
    copies[0].wait()
    sources = [before_ref[0], latent_ref[0], latent_ref[1], after_ref[0]]
    for r, source in enumerate(sources):
        value = (source.astype(F32) - mean) * rate * gain + bias
        act = value / (1.0 + jnp.exp(-value))
        if r == 0:
            act = act * vec_ref[5:6]
        if r == 3:
            act = act * vec_ref[6:7]
        here = slice(128 * r, 128 * r + 128)
        left = jnp.where(row == 0, 0.0, pltpu.roll(act, 1, 0))
        right = jnp.where(row == 127, 0.0, pltpu.roll(act, 127, 0))
        shift_ref[0, here] = left.astype(BF16)
        shift_ref[1, here] = act.astype(BF16)
        shift_ref[2, here] = right.astype(BF16)
    total = latent_ref[...].reshape(256, chans).astype(F32) + conv_bias
    for i in range(3):
        copies[1 + i].wait()
        for col in range(3):
            total = total + dot(shift_ref[col, 128 * i : 128 * i + 256, :], conv_ref[i, col])
    hidden = total.astype(BF16)
    hidden_ref[...] = hidden
    values = hidden.astype(F32)
    values = values - jnp.mean(values, axis=1, keepdims=True)
    spread = jnp.mean(values * values, axis=1, keepdims=True)
    normed = (values * lax.rsqrt(spread + 1e-05) * ln_gain + ln_bias).astype(BF16)
    scale = math.log2(math.e) / math.sqrt(HEAD_DIM)
    copies[4].wait()
    query = (dot(normed, w_ref[0]) * scale).astype(BF16)
    copies[5].wait()
    key = dot(normed, w_ref[1]).T.astype(BF16)
    copies[6].wait()
    value = dot(normed, w_ref[2]).astype(BF16)
    for s in range(SETS):
        main, extra, part = 64 * s, 64 * (SETS + s // 4), 64 * (s % 4)
        send_ref[s, 0:256] = jnp.concatenate(
            [query[:, main : main + 64], query[:, extra : extra + 64]], axis=1
        )
        send_ref[s, 256:320] = key[main : main + 64, 0:128]
        send_ref[s, 320:384] = key[main : main + 64, 128:256]
        send_ref[s, 384:512] = jnp.concatenate(
            [value[0:128, main : main + 64], value[128:256, main : main + 64]], axis=1
        )
        send_ref[s, 512:576] = jnp.concatenate(
            [key[extra : extra + 64, part : part + 64], value[part : part + 64, extra : extra + 64]],
            axis=1,
        )


def front(sums, vec, before, after, latent, conv_weight, w_query, w_key, w_value):
    chans = latent.shape[2]
    far = [latent, conv_weight, w_query, w_key, w_value]
    far = [pltpu.with_memory_space_constraint(a, pltpu.HBM) for a in far]
    return pl.pallas_call(
        front_kernel,
        in_specs=[pl.BlockSpec(memory_space=pltpu.VMEM)] * 4
        + [pl.BlockSpec(memory_space=pltpu.HBM)] * 5,
        out_specs=[pl.BlockSpec(memory_space=pltpu.VMEM)] * 2,
        out_shape=[
            jax.ShapeDtypeStruct((256, chans), BF16),
            jax.ShapeDtypeStruct((SETS, SEND_ROWS, LANES), BF16),
        ],
        scratch_shapes=[
            pltpu.VMEM((3, 512, chans), BF16),
            pltpu.VMEM(latent.shape, BF16),
            pltpu.VMEM(conv_weight.shape, BF16),
            pltpu.VMEM((3, chans, chans), BF16),
            pltpu.SemaphoreType.DMA((7,)),
        ],
        compiler_params=VMEM,
        name="front",
    )(sums, vec, before, after, *far)


def main_step(kv_ref, pair):
    lane = lanes(128)
    keys, values = [], []
    for src in (2 * pair, 2 * pair + 1):
        keys += [kv_ref[src, 0:64, :], kv_ref[src, 64:128, :]]
        value = kv_ref[src, 128:256, :]
        for side in (value, swap(value)):
            values.append(jnp.where(lane < 64, side, jnp.ones_like(side)))
    keys = jnp.concatenate([jnp.concatenate(keys, axis=1), jnp.zeros((64, SPAN), BF16)], axis=0)
    return 0, keys, jnp.concatenate(values, axis=0)


def extra_step(kv_ref, block):
    lane = lanes(64)
    sources = [SETS * block + src for src in range(SETS)]
    keys = [kv_ref[src, 256:320, 0:64] for src in sources]
    values = [kv_ref[src, 256:320, :] for src in sources]
    values = [jnp.where(lane >= 64, v, jnp.ones_like(v)) for v in values]
    keys = jnp.concatenate([jnp.zeros((64, SPAN), BF16), jnp.concatenate(keys, axis=1)], axis=0)
    return 1, keys, jnp.concatenate(values, axis=0)


def fold_kernel(count, tile, first, last, q_ref, *refs):
    block = pl.program_id(1)
    kv_refs, refs = refs[:count], refs[count:]
    if not first:
        acc_in, refs = refs[0], refs[1:]
    if last:
        far_refs, refs = refs[:SETS], refs[SETS:]
    acc_ref = refs[0]
    if count == 1:
        kv_ref = kv_refs[0]
    else:
        kv_ref = refs[-1]
        for i in range(count):

            @pl.when(block == i)
            def _():
                kv_ref[...] = kv_refs[i][...]

    @pl.when(block == 0)
    def _():
        acc_ref[...] = jnp.zeros(acc_ref.shape, F32) if first else acc_in[...]

    query = q_ref[...].reshape(tile, LANES)

    steps = [functools.partial(main_step, kv_ref, pair) for pair in range(SETS // 2)]
    steps.append(functools.partial(extra_step, kv_ref, 0))
    held = None
    for step in steps + [None]:
        if step is not None:
            kind, keys, values = step()
            score = dot(query, keys)
        if held is not None:
            held_kind, held_score, held_values = held
            weight = jnp.exp2(held_score).astype(BF16)
            acc_ref[0, held_kind] += dot(weight, held_values)
        held = None if step is None else (kind, score, values)

    if last:
        out_ref, store_ref, top_ref, sems = refs[1:]
        wide = lanes(tile)
        total = jnp.where(wide < 64, acc_ref[0, 1], acc_ref[0, 0])
        good = (jnp.min(total) > LOW) & (jnp.max(total) < HIGH)
        top_ref[...] = jnp.zeros((2, tile, LANES), F32)

        @pl.when(jnp.logical_not(good))
        def _():
            copies = []
            for i, far_ref in enumerate(far_refs):
                here = store_ref.at[pl.ds(SETS * i, SETS)]
                copies.append(pltpu.make_async_copy(far_ref, here, sems.at[i]))
                copies[-1].start()
            acc_ref[...] = jnp.zeros(acc_ref.shape, F32)
            top_ref[...] = jnp.full((2, tile, LANES), -1e30, F32)
            for copy in copies:
                copy.wait()

            def online(step):
                kind, keys, values = step
                score = dot(query, keys)
                top = jnp.maximum(top_ref[kind], jnp.max(score, axis=1, keepdims=True))
                weight = jnp.exp2(score - top[:, 0:1]).astype(BF16)
                factor = jnp.exp2(top_ref[kind] - top)
                acc_ref[0, kind] = acc_ref[0, kind] * factor + dot(weight, values)
                top_ref[kind] = top

            def pair_body(pair, carry):
                online(main_step(store_ref, pair))
                return carry

            def block_body(block, carry):
                online(extra_step(store_ref, block))
                return carry

            lax.fori_loop(0, SETS * SETS // 2, pair_body, 0)
            lax.fori_loop(0, SETS, block_body, 0)

        main, extra = acc_ref[0, 0], acc_ref[0, 1]
        out = jnp.where(wide < 64, main, extra) / jnp.where(wide < 64, swap(main), swap(extra))
        out = out.astype(BF16)
        level = (jnp.log2(extra) + top_ref[1])[:, 0:1]
        row = lax.broadcasted_iota(jnp.int32, (16, LANES), 0)
        for src in range(tile // 256):
            out_ref[src, 0:256] = out[256 * src : 256 * src + 256]
            tail = jnp.zeros((16, LANES), F32)
            for half in range(2):
                base = 256 * src + 128 * half
                line = jnp.broadcast_to(level[base : base + 128], (128, LANES)).T[0:16]
                for part in range(3):
                    piece = line.astype(BF16).astype(F32)
                    tail = jnp.where(row == 2 * part + half, piece, tail)
                    line = line - piece
            out_ref[src, 256:272] = tail.astype(BF16)


def fold(got, blocks, acc, every=None, tile=1024):
    per = ACC // tile
    first, last = acc is None, every is not None
    acc_spec = pl.BlockSpec((1, 2, tile, LANES), lambda t, b: (t // per, 0, t % per, 0))
    kv_spec = pl.BlockSpec((SETS, KV_ROWS, LANES), lambda t, b: (0, 0, 0))
    out_specs = [acc_spec]
    out_shape = [jax.ShapeDtypeStruct((TOKENS // ACC, 2, ACC, LANES), F32)]
    scratch = [pltpu.VMEM(blocks[0].shape, BF16)] if len(blocks) > 1 else []
    if last:
        out_specs.append(pl.BlockSpec((tile // 256, BACK_ROWS, LANES), lambda t, b: (t, 0, 0)))
        out_shape.append(jax.ShapeDtypeStruct((SETS, BACK_ROWS, LANES), BF16))
        scratch = [
            pltpu.VMEM((SETS * SETS, KV_ROWS, LANES), BF16),
            pltpu.VMEM((2, tile, LANES), F32),
            pltpu.SemaphoreType.DMA((SETS,)),
        ]
    return pl.pallas_call(
        functools.partial(fold_kernel, len(blocks), tile, first, last),
        grid=(TOKENS // tile, len(blocks)),
        in_specs=[pl.BlockSpec((tile // 256, Q_ROWS, LANES), lambda t, b: (t, 0, 0))]
        + [kv_spec] * len(blocks)
        + ([] if first else [acc_spec])
        + ([pl.BlockSpec(memory_space=pl.ANY)] * SETS if last else []),
        out_specs=out_specs,
        out_shape=out_shape,
        scratch_shapes=scratch,
        input_output_aliases={} if first else {1 + len(blocks): 0},
        compiler_params=VMEM,
        name="fold",
    )(got, *blocks, *(() if first else (acc,)), *(every or ()))


def finish_kernel(back_ref, hidden_ref, out_ref):
    for pair in range(SETS // 2):
        here = slice(128 * pair, 128 * pair + 128)
        both = [back_ref[2 * pair, 0:256, 0:64], back_ref[2 * pair + 1, 0:256, 0:64]]
        both = jnp.concatenate(both, axis=1).astype(F32)
        out_ref[:, here] = (hidden_ref[:, here].astype(F32) + both).astype(BF16)
    for half in range(2):
        rows = slice(128 * half, 128 * half + 128)
        shares = []
        for head in range(2):
            levels = []
            for s in range(4 * head, 4 * head + 4):
                tail = back_ref[s, 256:272].astype(F32)
                levels.append(sum(tail[2 * p + half : 2 * p + half + 1] for p in range(3)))
            top = functools.reduce(jnp.maximum, levels)
            parts = [jnp.exp2(level - top) for level in levels]
            total = sum(parts)
            shares += [part / total for part in parts]
        table = jnp.concatenate(shares + [jnp.zeros((LANES - SETS, LANES), F32)], axis=0).T
        both = []
        for head in range(2):
            value = jnp.zeros((128, 64), F32)
            for s in range(4 * head, 4 * head + 4):
                part = back_ref[s, rows, 64:128].astype(F32)
                value = value + part * jnp.broadcast_to(table[:, s : s + 1], (128, 64))
            both.append(value)
        here = slice(64 * SETS, 64 * SETS + 128)
        value = hidden_ref[rows, here].astype(F32) + jnp.concatenate(both, axis=1)
        out_ref[rows, here] = value.astype(BF16)


def finish(back, hidden):
    return pl.pallas_call(
        finish_kernel,
        in_specs=[pl.BlockSpec(memory_space=pltpu.VMEM)] * 2,
        out_specs=pl.BlockSpec(memory_space=pltpu.VMEM),
        out_shape=jax.ShapeDtypeStruct(hidden.shape, BF16),
        name="finish",
    )(*[pltpu.with_memory_space_constraint(a, pltpu.VMEM) for a in (back, hidden)])


def on_device(
    latent, gn_gain, gn_bias, conv_weight, conv_bias, ln_gain, ln_bias, w_query, w_key, w_value
):
    rows_here, cols, chans = latent.shape
    width = chans // GROUPS
    sums, last, first = begin(latent)
    before, after = halo(last, first)
    sums = total_of(sums)
    sums = jnp.sum(sums.reshape(2, GROUPS, width), axis=2, keepdims=True)
    sums = jnp.broadcast_to(sums, (2, GROUPS, width)).reshape(2, chans)
    place = lax.axis_index(BAND)
    row = lax.broadcasted_iota(jnp.int32, (8, chans), 0)
    vec = jnp.where(row == 5, jnp.where(place > 0, 1.0, 0.0), 0.0)
    vec = jnp.where(row == 6, jnp.where(place < BANDS - 1, 1.0, 0.0), vec)
    for i, part in enumerate((gn_gain, gn_bias, conv_bias, ln_gain, ln_bias)):
        vec = jnp.where(row == i, part, vec)
    hidden, send = front(
        sums, vec, before, after, latent, conv_weight, w_query, w_key, w_value
    )

    got = lax.all_to_all(send, ("x", "z"), 0, 0)
    own = got[:, Q_ROWS:]
    spots = [(y, c) for y in range(NY) for c in range(NC)]
    along = [(2 * y + c, 2 * ((y + 1 - 2 * c) % NY) + c) for y, c in spots]
    against = [(j, i) for i, j in along]
    cross = [(2 * y + c, 2 * y + 1 - c) for y, c in spots]

    tied = lax.optimization_barrier
    twin = lax.ppermute(own, RING, cross)
    ahead = lax.ppermute(own, RING, along)
    behind = lax.ppermute(own, RING, against)
    (acc,) = fold(got, [own, twin], None)
    ahead, acc = tied((ahead, acc))
    ahead_twin = lax.ppermute(ahead, RING, cross)
    far = lax.ppermute(ahead, RING, along)
    (acc,) = fold(got, [ahead], acc)
    behind, acc = tied((behind, acc))
    behind_twin = lax.ppermute(behind, RING, cross)
    (acc,) = fold(got, [behind, ahead_twin], acc)
    far, acc = tied((far, acc))
    far_twin = lax.ppermute(far, RING, cross)
    (acc,) = fold(got, [behind_twin, far], acc)
    every = [own, twin, ahead, behind, ahead_twin, behind_twin, far, far_twin]
    unused, out = fold(got, [far_twin], acc, every)

    back = lax.all_to_all(out, ("x", "z"), 0, 0)
    return finish(back, hidden).reshape(rows_here, cols, chans)


def solution(mesh):
    inner = Mesh(mesh.devices.reshape(NX, NZ, NY, NC, -1), BAND + ("img",))
    place = P(("img",) + BAND, None, None)
    in_specs = (place,) + (P(),) * 9
    return jax.shard_map(
        on_device, mesh=inner, in_specs=in_specs, out_specs=place, check_vma=False
    )
```

```python
import functools
import math

import jax
import jax.numpy as jnp
from jax import lax
from jax.experimental import pallas as pl
from jax.experimental.pallas import tpu as pltpu
from jax.sharding import Mesh
from jax.sharding import PartitionSpec as P

HEADS = 10
HEAD_DIM = 64
GROUPS = 16
NX, NZ, NY, NC = (4, 2, 4, 2)
BAND = ("x", "z", "y", "core")
RING = ("y", "core")
SETS = NX * NZ
BANDS = NX * NZ * NY * NC
SPAN = 512
TOKENS = 2048
ACC = 1024
LANES = 128
Q_ROWS = 256
KV_ROWS = 320
SEND_ROWS = Q_ROWS + KV_ROWS
BACK_ROWS = 272
HIGH = 2.0**100
LOW = 2.0**-60
BF16 = jnp.bfloat16
F32 = jnp.float32
VMEM = pltpu.CompilerParams(vmem_limit_bytes=24 * 1024 * 1024)


def total_of(value):
    for axis, size in (("y", NY), (("z", "core"), NZ * NC), ("x", NX)):
        parts = [value]
        for step in range(1, size):
            perm = [(i, (i + step) % size) for i in range(size)]
            parts.append(lax.ppermute(value, axis, perm))
        value = sum(parts[1:], parts[0])
    return value


def halo(last, first):
    up = [(i, i + 1) for i in range(BANDS - 1)]
    down = [(j, i) for i, j in up]
    before = lax.ppermute(last, BAND, up)
    after = lax.ppermute(first, BAND, down)
    return before, after


def dot(a, b):
    return jnp.dot(a, b, preferred_element_type=F32)


def swap(a):
    return jnp.concatenate([a[:, 64:128], a[:, 0:64]], axis=1)


def lanes(rows):
    return lax.broadcasted_iota(jnp.int32, (rows, LANES), 1)


def begin_kernel(latent_hbm, sums_ref, last_ref, first_ref, latent_ref, sem):
    copy = pltpu.make_async_copy(latent_hbm, latent_ref, sem.at[0])
    copy.start()
    copy.wait()
    first, last = latent_ref[0].astype(F32), latent_ref[1].astype(F32)
    sums_ref[0:1] = jnp.sum(first + last, axis=0, keepdims=True)
    sums_ref[1:2] = jnp.sum(first * first + last * last, axis=0, keepdims=True)
    last_ref[0] = latent_ref[1]
    first_ref[0] = latent_ref[0]


def begin(latent):
    edge = jax.ShapeDtypeStruct((1,) + latent.shape[1:], BF16)
    return pl.pallas_call(
        begin_kernel,
        in_specs=[pl.BlockSpec(memory_space=pltpu.HBM)],
        out_specs=[pl.BlockSpec(memory_space=pltpu.VMEM)] * 3,
        out_shape=[pltpu.VMEM((2, latent.shape[2]), F32), edge, edge],
        scratch_shapes=[pltpu.VMEM(latent.shape, BF16), pltpu.SemaphoreType.DMA((1,))],
        name="begin",
    )(pltpu.with_memory_space_constraint(latent, pltpu.HBM))


def front_kernel(
    sums_ref, vec_ref, before_ref, after_ref, latent_hbm, conv_hbm, wq_hbm, wk_hbm, wv_hbm,
    hidden_ref, send_ref, shift_ref, latent_ref, conv_ref, w_ref, sems,
):
    copies = [pltpu.make_async_copy(latent_hbm, latent_ref, sems.at[0])]
    for i in range(3):
        copies.append(pltpu.make_async_copy(conv_hbm.at[i], conv_ref.at[i], sems.at[1 + i]))
    for i, w_hbm in enumerate((wq_hbm, wk_hbm, wv_hbm)):
        copies.append(pltpu.make_async_copy(w_hbm, w_ref.at[i], sems.at[4 + i]))
    for copy in copies:
        copy.start()
    chans = latent_ref.shape[2]
    count = float(BANDS * 256 * (chans // GROUPS))
    mean = sums_ref[0:1] / count
    var = sums_ref[1:2] / count - mean * mean
    rate = lax.rsqrt(var + 1e-05)
    gain, bias, conv_bias, ln_gain, ln_bias = [vec_ref[i : i + 1] for i in range(5)]
    row = lax.broadcasted_iota(jnp.int32, (128, chans), 0)
    copies[0].wait()
    sources = [before_ref[0], latent_ref[0], latent_ref[1], after_ref[0]]
    for r, source in enumerate(sources):
        value = (source.astype(F32) - mean) * rate * gain + bias
        act = value / (1.0 + jnp.exp(-value))
        if r == 0:
            act = act * vec_ref[5:6]
        if r == 3:
            act = act * vec_ref[6:7]
        here = slice(128 * r, 128 * r + 128)
        left = jnp.where(row == 0, 0.0, pltpu.roll(act, 1, 0))
        right = jnp.where(row == 127, 0.0, pltpu.roll(act, 127, 0))
        shift_ref[0, here] = left.astype(BF16)
        shift_ref[1, here] = act.astype(BF16)
        shift_ref[2, here] = right.astype(BF16)
    total = latent_ref[...].reshape(256, chans).astype(F32) + conv_bias
    for i in range(3):
        copies[1 + i].wait()
        for col in range(3):
            total = total + dot(shift_ref[col, 128 * i : 128 * i + 256, :], conv_ref[i, col])
    hidden = total.astype(BF16)
    hidden_ref[...] = hidden
    values = hidden.astype(F32)
    values = values - jnp.mean(values, axis=1, keepdims=True)
    spread = jnp.mean(values * values, axis=1, keepdims=True)
    normed = (values * lax.rsqrt(spread + 1e-05) * ln_gain + ln_bias).astype(BF16)
    scale = math.log2(math.e) / math.sqrt(HEAD_DIM)
    copies[4].wait()
    query = (dot(normed, w_ref[0]) * scale).astype(BF16)
    copies[5].wait()
    key = dot(normed, w_ref[1]).T.astype(BF16)
    copies[6].wait()
    value = dot(normed, w_ref[2]).astype(BF16)
    for s in range(SETS):
        main, extra, part = 64 * s, 64 * (SETS + s // 4), 64 * (s % 4)
        send_ref[s, 0:256] = jnp.concatenate(
            [query[:, main : main + 64], query[:, extra : extra + 64]], axis=1
        )
        send_ref[s, 256:320] = key[main : main + 64, 0:128]
        send_ref[s, 320:384] = key[main : main + 64, 128:256]
        send_ref[s, 384:512] = jnp.concatenate(
            [value[0:128, main : main + 64], value[128:256, main : main + 64]], axis=1
        )
        send_ref[s, 512:576] = jnp.concatenate(
            [key[extra : extra + 64, part : part + 64], value[part : part + 64, extra : extra + 64]],
            axis=1,
        )


def front(sums, vec, before, after, latent, conv_weight, w_query, w_key, w_value):
    chans = latent.shape[2]
    far = [latent, conv_weight, w_query, w_key, w_value]
    far = [pltpu.with_memory_space_constraint(a, pltpu.HBM) for a in far]
    return pl.pallas_call(
        front_kernel,
        in_specs=[pl.BlockSpec(memory_space=pltpu.VMEM)] * 4
        + [pl.BlockSpec(memory_space=pltpu.HBM)] * 5,
        out_specs=[pl.BlockSpec(memory_space=pltpu.VMEM)] * 2,
        out_shape=[
            jax.ShapeDtypeStruct((256, chans), BF16),
            jax.ShapeDtypeStruct((SETS, SEND_ROWS, LANES), BF16),
        ],
        scratch_shapes=[
            pltpu.VMEM((3, 512, chans), BF16),
            pltpu.VMEM(latent.shape, BF16),
            pltpu.VMEM(conv_weight.shape, BF16),
            pltpu.VMEM((3, chans, chans), BF16),
            pltpu.SemaphoreType.DMA((7,)),
        ],
        compiler_params=VMEM,
        name="front",
    )(sums, vec, before, after, *far)


def main_step(kv_ref, pair):
    lane = lanes(128)
    keys, values = [], []
    for src in (2 * pair, 2 * pair + 1):
        keys += [kv_ref[src, 0:64, :], kv_ref[src, 64:128, :]]
        value = kv_ref[src, 128:256, :]
        for side in (value, swap(value)):
            values.append(jnp.where(lane < 64, side, jnp.ones_like(side)))
    keys = jnp.concatenate([jnp.concatenate(keys, axis=1), jnp.zeros((64, SPAN), BF16)], axis=0)
    return 0, keys, jnp.concatenate(values, axis=0)


def extra_step(kv_ref, block):
    lane = lanes(64)
    sources = [SETS * block + src for src in range(SETS)]
    keys = [kv_ref[src, 256:320, 0:64] for src in sources]
    values = [kv_ref[src, 256:320, :] for src in sources]
    values = [jnp.where(lane >= 64, v, jnp.ones_like(v)) for v in values]
    keys = jnp.concatenate([jnp.zeros((64, SPAN), BF16), jnp.concatenate(keys, axis=1)], axis=0)
    return 1, keys, jnp.concatenate(values, axis=0)


def fold_kernel(count, tile, first, last, q_ref, *refs):
    block = pl.program_id(1)
    kv_refs, refs = refs[:count], refs[count:]
    if not first:
        acc_in, refs = refs[0], refs[1:]
    if last:
        far_refs, refs = refs[:SETS], refs[SETS:]
    acc_ref = refs[0]
    if count == 1:
        kv_ref = kv_refs[0]
    else:
        kv_ref = refs[-1]
        for i in range(count):

            @pl.when(block == i)
            def _():
                kv_ref[...] = kv_refs[i][...]

    @pl.when(block == 0)
    def _():
        acc_ref[...] = jnp.zeros(acc_ref.shape, F32) if first else acc_in[...]

    query = q_ref[...].reshape(tile, LANES)

    steps = [functools.partial(main_step, kv_ref, pair) for pair in range(SETS // 2)]
    steps.append(functools.partial(extra_step, kv_ref, 0))
    held = None
    for step in steps + [None]:
        if step is not None:
            kind, keys, values = step()
            score = dot(query, keys)
        if held is not None:
            held_kind, held_score, held_values = held
            weight = jnp.exp2(held_score).astype(BF16)
            acc_ref[0, held_kind] += dot(weight, held_values)
        held = None if step is None else (kind, score, values)

    if last:
        out_ref, store_ref, top_ref, sems = refs[1:5]

        @pl.when(block == count - 1)
        def _():
            wide = lanes(tile)
            total = jnp.where(wide < 64, acc_ref[0, 1], acc_ref[0, 0])
            good = (jnp.min(total) > LOW) & (jnp.max(total) < HIGH)
            top_ref[...] = jnp.zeros((2, tile, LANES), F32)

            @pl.when(jnp.logical_not(good))
            def _():
                copies = []
                for i, far_ref in enumerate(far_refs):
                    here = store_ref.at[pl.ds(SETS * i, SETS)]
                    copies.append(pltpu.make_async_copy(far_ref, here, sems.at[i]))
                    copies[-1].start()
                acc_ref[...] = jnp.zeros(acc_ref.shape, F32)
                top_ref[...] = jnp.full((2, tile, LANES), -1e30, F32)
                for copy in copies:
                    copy.wait()

                def online(step):
                    kind, keys, values = step
                    score = dot(query, keys)
                    top = jnp.maximum(top_ref[kind], jnp.max(score, axis=1, keepdims=True))
                    weight = jnp.exp2(score - top[:, 0:1]).astype(BF16)
                    factor = jnp.exp2(top_ref[kind] - top)
                    acc_ref[0, kind] = acc_ref[0, kind] * factor + dot(weight, values)
                    top_ref[kind] = top

                def pair_body(pair, carry):
                    online(main_step(store_ref, pair))
                    return carry

                def block_body(block, carry):
                    online(extra_step(store_ref, block))
                    return carry

                lax.fori_loop(0, SETS * SETS // 2, pair_body, 0)
                lax.fori_loop(0, SETS, block_body, 0)

            main, extra = acc_ref[0, 0], acc_ref[0, 1]
            out = jnp.where(wide < 64, main, extra) / jnp.where(wide < 64, swap(main), swap(extra))
            out = out.astype(BF16)
            level = (jnp.log2(extra) + top_ref[1])[:, 0:1]
            row = lax.broadcasted_iota(jnp.int32, (16, LANES), 0)
            for src in range(tile // 256):
                out_ref[src, 0:256] = out[256 * src : 256 * src + 256]
                tail = jnp.zeros((16, LANES), F32)
                for half in range(2):
                    base = 256 * src + 128 * half
                    line = jnp.broadcast_to(level[base : base + 128], (128, LANES)).T[0:16]
                    for part in range(3):
                        piece = line.astype(BF16).astype(F32)
                        tail = jnp.where(row == 2 * part + half, piece, tail)
                        line = line - piece
                out_ref[src, 256:272] = tail.astype(BF16)


def fold(got, blocks, acc, every=None, tile=1024):
    per = ACC // tile
    first, last = acc is None, every is not None
    acc_spec = pl.BlockSpec((1, 2, tile, LANES), lambda t, b: (t // per, 0, t % per, 0))
    kv_spec = pl.BlockSpec((SETS, KV_ROWS, LANES), lambda t, b: (0, 0, 0))
    out_specs = [acc_spec]
    out_shape = [jax.ShapeDtypeStruct((TOKENS // ACC, 2, ACC, LANES), F32)]
    scratch = [pltpu.VMEM(blocks[0].shape, BF16)] if len(blocks) > 1 else []
    if last:
        out_specs.append(pl.BlockSpec((tile // 256, BACK_ROWS, LANES), lambda t, b: (t, 0, 0)))
        out_shape.append(jax.ShapeDtypeStruct((SETS, BACK_ROWS, LANES), BF16))
        scratch = [
            pltpu.VMEM((SETS * SETS, KV_ROWS, LANES), BF16),
            pltpu.VMEM((2, tile, LANES), F32),
            pltpu.SemaphoreType.DMA((SETS,)),
        ] + scratch
    return pl.pallas_call(
        functools.partial(fold_kernel, len(blocks), tile, first, last),
        grid=(TOKENS // tile, len(blocks)),
        in_specs=[pl.BlockSpec((tile // 256, Q_ROWS, LANES), lambda t, b: (t, 0, 0))]
        + [kv_spec] * len(blocks)
        + ([] if first else [acc_spec])
        + ([pl.BlockSpec(memory_space=pl.ANY)] * SETS if last else []),
        out_specs=out_specs,
        out_shape=out_shape,
        scratch_shapes=scratch,
        input_output_aliases={} if first else {1 + len(blocks): 0},
        compiler_params=VMEM,
        name="fold",
    )(got, *blocks, *(() if first else (acc,)), *(every or ()))


def finish_kernel(back_ref, hidden_ref, out_ref):
    for pair in range(SETS // 2):
        here = slice(128 * pair, 128 * pair + 128)
        both = [back_ref[2 * pair, 0:256, 0:64], back_ref[2 * pair + 1, 0:256, 0:64]]
        both = jnp.concatenate(both, axis=1).astype(F32)
        out_ref[:, here] = (hidden_ref[:, here].astype(F32) + both).astype(BF16)
    for half in range(2):
        rows = slice(128 * half, 128 * half + 128)
        shares = []
        for head in range(2):
            levels = []
            for s in range(4 * head, 4 * head + 4):
                tail = back_ref[s, 256:272].astype(F32)
                levels.append(sum(tail[2 * p + half : 2 * p + half + 1] for p in range(3)))
            top = functools.reduce(jnp.maximum, levels)
            parts = [jnp.exp2(level - top) for level in levels]
            total = sum(parts)
            shares += [part / total for part in parts]
        table = jnp.concatenate(shares + [jnp.zeros((LANES - SETS, LANES), F32)], axis=0).T
        both = []
        for head in range(2):
            value = jnp.zeros((128, 64), F32)
            for s in range(4 * head, 4 * head + 4):
                part = back_ref[s, rows, 64:128].astype(F32)
                value = value + part * jnp.broadcast_to(table[:, s : s + 1], (128, 64))
            both.append(value)
        here = slice(64 * SETS, 64 * SETS + 128)
        value = hidden_ref[rows, here].astype(F32) + jnp.concatenate(both, axis=1)
        out_ref[rows, here] = value.astype(BF16)


def finish(back, hidden):
    return pl.pallas_call(
        finish_kernel,
        in_specs=[pl.BlockSpec(memory_space=pltpu.VMEM)] * 2,
        out_specs=pl.BlockSpec(memory_space=pltpu.VMEM),
        out_shape=jax.ShapeDtypeStruct(hidden.shape, BF16),
        name="finish",
    )(*[pltpu.with_memory_space_constraint(a, pltpu.VMEM) for a in (back, hidden)])


def on_device(
    latent, gn_gain, gn_bias, conv_weight, conv_bias, ln_gain, ln_bias, w_query, w_key, w_value
):
    rows_here, cols, chans = latent.shape
    width = chans // GROUPS
    sums, last, first = begin(latent)
    before, after = halo(last, first)
    sums = total_of(sums)
    sums = jnp.sum(sums.reshape(2, GROUPS, width), axis=2, keepdims=True)
    sums = jnp.broadcast_to(sums, (2, GROUPS, width)).reshape(2, chans)
    place = lax.axis_index(BAND)
    row = lax.broadcasted_iota(jnp.int32, (8, chans), 0)
    vec = jnp.where(row == 5, jnp.where(place > 0, 1.0, 0.0), 0.0)
    vec = jnp.where(row == 6, jnp.where(place < BANDS - 1, 1.0, 0.0), vec)
    for i, part in enumerate((gn_gain, gn_bias, conv_bias, ln_gain, ln_bias)):
        vec = jnp.where(row == i, part, vec)
    hidden, send = front(
        sums, vec, before, after, latent, conv_weight, w_query, w_key, w_value
    )

    got = lax.all_to_all(send, ("x", "z"), 0, 0)
    own = got[:, Q_ROWS:]
    spots = [(y, c) for y in range(NY) for c in range(NC)]
    along = [(2 * y + c, 2 * ((y + 1 - 2 * c) % NY) + c) for y, c in spots]
    against = [(j, i) for i, j in along]
    cross = [(2 * y + c, 2 * y + 1 - c) for y, c in spots]

    tied = lax.optimization_barrier
    twin = lax.ppermute(own, RING, cross)
    ahead = lax.ppermute(own, RING, along)
    (acc,) = fold(got, [own, twin], None)
    own, ahead, acc = tied((own, ahead, acc))
    ahead_twin = lax.ppermute(ahead, RING, cross)
    behind = lax.ppermute(own, RING, against)
    far = lax.ppermute(ahead, RING, along)
    (acc,) = fold(got, [ahead, ahead_twin], acc)
    behind, far, acc = tied((behind, far, acc))
    behind_twin = lax.ppermute(behind, RING, cross)
    far_twin = lax.ppermute(far, RING, cross)
    (acc,) = fold(got, [behind, far], acc)
    every = [own, twin, ahead, behind, ahead_twin, behind_twin, far, far_twin]
    unused, out = fold(got, [behind_twin, far_twin], acc, every)

    back = lax.all_to_all(out, ("x", "z"), 0, 0)
    return finish(back, hidden).reshape(rows_here, cols, chans)


def solution(mesh):
    inner = Mesh(mesh.devices.reshape(NX, NZ, NY, NC, -1), BAND + ("img",))
    place = P(("img",) + BAND, None, None)
    in_specs = (place,) + (P(),) * 9
    return jax.shard_map(
        on_device, mesh=inner, in_specs=in_specs, out_specs=place, check_vma=False
    )
```

```python
import functools
import math

import jax
import jax.numpy as jnp
from jax import lax
from jax.experimental import pallas as pl
from jax.experimental.pallas import tpu as pltpu
from jax.sharding import Mesh
from jax.sharding import PartitionSpec as P

HEADS = 10
HEAD_DIM = 64
GROUPS = 16
NX, NZ, NY, NC = (4, 2, 4, 2)
BAND = ("x", "z", "y", "core")
RING = ("y", "core")
SETS = NX * NZ
BANDS = NX * NZ * NY * NC
SPAN = 512
TOKENS = 2048
LANES = 128
Q_ROWS = 256
KV_ROWS = 320
SEND_ROWS = Q_ROWS + KV_ROWS
BACK_ROWS = 272
HIGH = 2.0**100
LOW = 2.0**-60
BF16 = jnp.bfloat16
F32 = jnp.float32
VMEM = pltpu.CompilerParams(vmem_limit_bytes=24 * 1024 * 1024)


def total_of(value):
    for axis, size in (("y", NY), (("z", "core"), NZ * NC), ("x", NX)):
        parts = [value]
        for step in range(1, size):
            perm = [(i, (i + step) % size) for i in range(size)]
            parts.append(lax.ppermute(value, axis, perm))
        value = sum(parts[1:], parts[0])
    return value


def halo(last, first):
    up = [(i, i + 1) for i in range(BANDS - 1)]
    down = [(j, i) for i, j in up]
    before = lax.ppermute(last, BAND, up)
    after = lax.ppermute(first, BAND, down)
    return before, after


def dot(a, b):
    return jnp.dot(a, b, preferred_element_type=F32)


def swap(a):
    return jnp.concatenate([a[:, 64:128], a[:, 0:64]], axis=1)


def lanes(rows):
    return lax.broadcasted_iota(jnp.int32, (rows, LANES), 1)


def begin_kernel(latent_hbm, sums_ref, last_ref, first_ref, latent_ref, sem):
    copy = pltpu.make_async_copy(latent_hbm, latent_ref, sem.at[0])
    copy.start()
    copy.wait()
    first, last = latent_ref[0].astype(F32), latent_ref[1].astype(F32)
    sums_ref[0:1] = jnp.sum(first + last, axis=0, keepdims=True)
    sums_ref[1:2] = jnp.sum(first * first + last * last, axis=0, keepdims=True)
    last_ref[0] = latent_ref[1]
    first_ref[0] = latent_ref[0]


def begin(latent):
    edge = jax.ShapeDtypeStruct((1,) + latent.shape[1:], BF16)
    return pl.pallas_call(
        begin_kernel,
        in_specs=[pl.BlockSpec(memory_space=pltpu.HBM)],
        out_specs=[pl.BlockSpec(memory_space=pltpu.VMEM)] * 3,
        out_shape=[pltpu.VMEM((2, latent.shape[2]), F32), edge, edge],
        scratch_shapes=[pltpu.VMEM(latent.shape, BF16), pltpu.SemaphoreType.DMA((1,))],
        name="begin",
    )(pltpu.with_memory_space_constraint(latent, pltpu.HBM))


def front_kernel(
    sums_ref, vec_ref, before_ref, after_ref, latent_hbm, conv_hbm, wq_hbm, wk_hbm, wv_hbm,
    hidden_ref, send_ref, shift_ref, latent_ref, conv_ref, w_ref, sems,
):
    copies = [pltpu.make_async_copy(latent_hbm, latent_ref, sems.at[0])]
    for i in range(3):
        copies.append(pltpu.make_async_copy(conv_hbm.at[i], conv_ref.at[i], sems.at[1 + i]))
    for i, w_hbm in enumerate((wq_hbm, wk_hbm, wv_hbm)):
        copies.append(pltpu.make_async_copy(w_hbm, w_ref.at[i], sems.at[4 + i]))
    for copy in copies:
        copy.start()
    chans = latent_ref.shape[2]
    count = float(BANDS * 256 * (chans // GROUPS))
    mean = sums_ref[0:1] / count
    var = sums_ref[1:2] / count - mean * mean
    rate = lax.rsqrt(var + 1e-05)
    gain, bias, conv_bias, ln_gain, ln_bias = [vec_ref[i : i + 1] for i in range(5)]
    row = lax.broadcasted_iota(jnp.int32, (128, chans), 0)
    copies[0].wait()
    sources = [before_ref[0], latent_ref[0], latent_ref[1], after_ref[0]]
    for r, source in enumerate(sources):
        value = (source.astype(F32) - mean) * rate * gain + bias
        act = value / (1.0 + jnp.exp(-value))
        if r == 0:
            act = act * vec_ref[5:6]
        if r == 3:
            act = act * vec_ref[6:7]
        here = slice(128 * r, 128 * r + 128)
        left = jnp.where(row == 0, 0.0, pltpu.roll(act, 1, 0))
        right = jnp.where(row == 127, 0.0, pltpu.roll(act, 127, 0))
        shift_ref[0, here] = left.astype(BF16)
        shift_ref[1, here] = act.astype(BF16)
        shift_ref[2, here] = right.astype(BF16)
    total = latent_ref[...].reshape(256, chans).astype(F32) + conv_bias
    for i in range(3):
        copies[1 + i].wait()
        for col in range(3):
            total = total + dot(shift_ref[col, 128 * i : 128 * i + 256, :], conv_ref[i, col])
    hidden = total.astype(BF16)
    hidden_ref[...] = hidden
    values = hidden.astype(F32)
    values = values - jnp.mean(values, axis=1, keepdims=True)
    spread = jnp.mean(values * values, axis=1, keepdims=True)
    normed = (values * lax.rsqrt(spread + 1e-05) * ln_gain + ln_bias).astype(BF16)
    scale = math.log2(math.e) / math.sqrt(HEAD_DIM)
    copies[4].wait()
    query = (dot(normed, w_ref[0]) * scale).astype(BF16)
    copies[5].wait()
    key = dot(normed, w_ref[1]).T.astype(BF16)
    copies[6].wait()
    value = dot(normed, w_ref[2]).astype(BF16)
    for s in range(SETS):
        main, extra, part = 64 * s, 64 * (SETS + s // 4), 64 * (s % 4)
        send_ref[s, 0:256] = jnp.concatenate(
            [query[:, main : main + 64], query[:, extra : extra + 64]], axis=1
        )
        send_ref[s, 256:320] = key[main : main + 64, 0:128]
        send_ref[s, 320:384] = key[main : main + 64, 128:256]
        send_ref[s, 384:512] = jnp.concatenate(
            [value[0:128, main : main + 64], value[128:256, main : main + 64]], axis=1
        )
        send_ref[s, 512:576] = jnp.concatenate(
            [key[extra : extra + 64, part : part + 64], value[part : part + 64, extra : extra + 64]],
            axis=1,
        )


def front(sums, vec, before, after, latent, conv_weight, w_query, w_key, w_value):
    chans = latent.shape[2]
    far = [latent, conv_weight, w_query, w_key, w_value]
    far = [pltpu.with_memory_space_constraint(a, pltpu.HBM) for a in far]
    return pl.pallas_call(
        front_kernel,
        in_specs=[pl.BlockSpec(memory_space=pltpu.VMEM)] * 4
        + [pl.BlockSpec(memory_space=pltpu.HBM)] * 5,
        out_specs=[pl.BlockSpec(memory_space=pltpu.VMEM)] * 2,
        out_shape=[
            jax.ShapeDtypeStruct((256, chans), BF16),
            jax.ShapeDtypeStruct((SETS, SEND_ROWS, LANES), BF16),
        ],
        scratch_shapes=[
            pltpu.VMEM((3, 512, chans), BF16),
            pltpu.VMEM(latent.shape, BF16),
            pltpu.VMEM(conv_weight.shape, BF16),
            pltpu.VMEM((3, chans, chans), BF16),
            pltpu.SemaphoreType.DMA((7,)),
        ],
        compiler_params=VMEM,
        name="front",
    )(sums, vec, before, after, *far)


def main_step(kv_ref, pair):
    lane = lanes(128)
    keys, values = [], []
    for src in (2 * pair, 2 * pair + 1):
        keys += [kv_ref[src, 0:64, :], kv_ref[src, 64:128, :]]
        value = kv_ref[src, 128:256, :]
        for side in (value, swap(value)):
            values.append(jnp.where(lane < 64, side, jnp.ones_like(side)))
    keys = jnp.concatenate([jnp.concatenate(keys, axis=1), jnp.zeros((64, SPAN), BF16)], axis=0)
    return 0, keys, jnp.concatenate(values, axis=0)


def extra_step(kv_ref, block):
    lane = lanes(64)
    sources = [SETS * block + src for src in range(SETS)]
    keys = [kv_ref[src, 256:320, 0:64] for src in sources]
    values = [kv_ref[src, 256:320, :] for src in sources]
    values = [jnp.where(lane >= 64, v, jnp.ones_like(v)) for v in values]
    keys = jnp.concatenate([jnp.zeros((64, SPAN), BF16), jnp.concatenate(keys, axis=1)], axis=0)
    return 1, keys, jnp.concatenate(values, axis=0)


def fold_kernel(count, tile, first, last, q_ref, *refs):
    kv_refs, refs = refs[:count], refs[count:]
    if not first:
        acc_in, refs = refs[0], refs[1:]
    if last:
        far_refs, refs = refs[:SETS], refs[SETS:]
    acc_ref = refs[0]
    acc_ref[...] = jnp.zeros(acc_ref.shape, F32) if first else acc_in[...]
    query = q_ref[...].reshape(tile, LANES)

    steps = []
    for kv_ref in kv_refs:
        steps += [functools.partial(main_step, kv_ref, pair) for pair in range(SETS // 2)]
        steps.append(functools.partial(extra_step, kv_ref, 0))
    held = None
    for step in steps + [None]:
        if step is not None:
            kind, keys, values = step()
            score = dot(query, keys)
        if held is not None:
            held_kind, held_score, held_values = held
            weight = jnp.exp2(held_score).astype(BF16)
            update = dot(weight, held_values)
            for i in range(tile // SPAN):
                acc_ref[i, held_kind] += update[SPAN * i : SPAN * i + SPAN]
        held = None if step is None else (kind, score, values)

    if last:
        out_ref, store_ref, top_ref, sems = refs[1:]
        wide = lanes(tile)
        total = jnp.where(wide < 64, acc_ref[0, 1], acc_ref[0, 0])
        good = (jnp.min(total) > LOW) & (jnp.max(total) < HIGH)
        top_ref[...] = jnp.zeros((2, tile, LANES), F32)

        @pl.when(jnp.logical_not(good))
        def _():
            copies = []
            for i, far_ref in enumerate(far_refs):
                here = store_ref.at[pl.ds(SETS * i, SETS)]
                copies.append(pltpu.make_async_copy(far_ref, here, sems.at[i]))
                copies[-1].start()
            acc_ref[...] = jnp.zeros(acc_ref.shape, F32)
            top_ref[...] = jnp.full((2, tile, LANES), -1e30, F32)
            for copy in copies:
                copy.wait()

            def online(step):
                kind, keys, values = step
                score = dot(query, keys)
                top = jnp.maximum(top_ref[kind], jnp.max(score, axis=1, keepdims=True))
                weight = jnp.exp2(score - top[:, 0:1]).astype(BF16)
                factor = jnp.exp2(top_ref[kind] - top)
                acc_ref[0, kind] = acc_ref[0, kind] * factor + dot(weight, values)
                top_ref[kind] = top

            def pair_body(pair, carry):
                online(main_step(store_ref, pair))
                return carry

            def block_body(block, carry):
                online(extra_step(store_ref, block))
                return carry

            lax.fori_loop(0, SETS * SETS // 2, pair_body, 0)
            lax.fori_loop(0, SETS, block_body, 0)

        main, extra = acc_ref[0, 0], acc_ref[0, 1]
        out = jnp.where(wide < 64, main, extra) / jnp.where(wide < 64, swap(main), swap(extra))
        out = out.astype(BF16)
        level = (jnp.log2(extra) + top_ref[1])[:, 0:1]
        row = lax.broadcasted_iota(jnp.int32, (16, LANES), 0)
        for src in range(tile // 256):
            out_ref[src, 0:256] = out[256 * src : 256 * src + 256]
            tail = jnp.zeros((16, LANES), F32)
            for half in range(2):
                base = 256 * src + 128 * half
                line = jnp.broadcast_to(level[base : base + 128], (128, LANES)).T[0:16]
                for part in range(3):
                    piece = line.astype(BF16).astype(F32)
                    tail = jnp.where(row == 2 * part + half, piece, tail)
                    line = line - piece
            out_ref[src, 256:272] = tail.astype(BF16)


def fold(got, blocks, acc, every=None, tile=SPAN):
    first, last = acc is None, every is not None
    acc_spec = pl.BlockSpec((tile // SPAN, 2, SPAN, LANES), lambda t: (t, 0, 0, 0))
    kv_spec = pl.BlockSpec((SETS, KV_ROWS, LANES), lambda t: (0, 0, 0))
    out_specs = [acc_spec]
    out_shape = [jax.ShapeDtypeStruct((TOKENS // SPAN, 2, SPAN, LANES), F32)]
    scratch = []
    if last:
        out_specs.append(pl.BlockSpec((tile // 256, BACK_ROWS, LANES), lambda t: (t, 0, 0)))
        out_shape.append(jax.ShapeDtypeStruct((SETS, BACK_ROWS, LANES), BF16))
        scratch = [
            pltpu.VMEM((SETS * SETS, KV_ROWS, LANES), BF16),
            pltpu.VMEM((2, tile, LANES), F32),
            pltpu.SemaphoreType.DMA((SETS,)),
        ]
    return pl.pallas_call(
        functools.partial(fold_kernel, len(blocks), tile, first, last),
        grid=(TOKENS // tile,),
        in_specs=[pl.BlockSpec((tile // 256, Q_ROWS, LANES), lambda t: (t, 0, 0))]
        + [kv_spec] * len(blocks)
        + ([] if first else [acc_spec])
        + ([pl.BlockSpec(memory_space=pl.ANY)] * SETS if last else []),
        out_specs=out_specs,
        out_shape=out_shape,
        scratch_shapes=scratch,
        input_output_aliases={} if first else {1 + len(blocks): 0},
        compiler_params=VMEM,
        name="fold",
    )(got, *blocks, *(() if first else (acc,)), *(every or ()))


def finish_kernel(back_ref, hidden_ref, out_ref):
    for pair in range(SETS // 2):
        here = slice(128 * pair, 128 * pair + 128)
        both = [back_ref[2 * pair, 0:256, 0:64], back_ref[2 * pair + 1, 0:256, 0:64]]
        both = jnp.concatenate(both, axis=1).astype(F32)
        out_ref[:, here] = (hidden_ref[:, here].astype(F32) + both).astype(BF16)
    for half in range(2):
        rows = slice(128 * half, 128 * half + 128)
        shares = []
        for head in range(2):
            levels = []
            for s in range(4 * head, 4 * head + 4):
                tail = back_ref[s, 256:272].astype(F32)
                levels.append(sum(tail[2 * p + half : 2 * p + half + 1] for p in range(3)))
            top = functools.reduce(jnp.maximum, levels)
            parts = [jnp.exp2(level - top) for level in levels]
            total = sum(parts)
            shares += [part / total for part in parts]
        table = jnp.concatenate(shares + [jnp.zeros((LANES - SETS, LANES), F32)], axis=0).T
        both = []
        for head in range(2):
            value = jnp.zeros((128, 64), F32)
            for s in range(4 * head, 4 * head + 4):
                part = back_ref[s, rows, 64:128].astype(F32)
                value = value + part * jnp.broadcast_to(table[:, s : s + 1], (128, 64))
            both.append(value)
        here = slice(64 * SETS, 64 * SETS + 128)
        value = hidden_ref[rows, here].astype(F32) + jnp.concatenate(both, axis=1)
        out_ref[rows, here] = value.astype(BF16)


def finish(back, hidden):
    return pl.pallas_call(
        finish_kernel,
        in_specs=[pl.BlockSpec(memory_space=pltpu.VMEM)] * 2,
        out_specs=pl.BlockSpec(memory_space=pltpu.VMEM),
        out_shape=jax.ShapeDtypeStruct(hidden.shape, BF16),
        name="finish",
    )(*[pltpu.with_memory_space_constraint(a, pltpu.VMEM) for a in (back, hidden)])


def on_device(
    latent, gn_gain, gn_bias, conv_weight, conv_bias, ln_gain, ln_bias, w_query, w_key, w_value
):
    rows_here, cols, chans = latent.shape
    width = chans // GROUPS
    sums, last, first = begin(latent)
    before, after = halo(last, first)
    sums = total_of(sums)
    sums = jnp.sum(sums.reshape(2, GROUPS, width), axis=2, keepdims=True)
    sums = jnp.broadcast_to(sums, (2, GROUPS, width)).reshape(2, chans)
    place = lax.axis_index(BAND)
    row = lax.broadcasted_iota(jnp.int32, (8, chans), 0)
    vec = jnp.where(row == 5, jnp.where(place > 0, 1.0, 0.0), 0.0)
    vec = jnp.where(row == 6, jnp.where(place < BANDS - 1, 1.0, 0.0), vec)
    for i, part in enumerate((gn_gain, gn_bias, conv_bias, ln_gain, ln_bias)):
        vec = jnp.where(row == i, part, vec)
    hidden, send = front(
        sums, vec, before, after, latent, conv_weight, w_query, w_key, w_value
    )

    got = lax.all_to_all(send, ("x", "z"), 0, 0)
    own = got[:, Q_ROWS:]
    spots = [(y, c) for y in range(NY) for c in range(NC)]
    along = [(2 * y + c, 2 * ((y + 1 - 2 * c) % NY) + c) for y, c in spots]
    against = [(j, i) for i, j in along]
    cross = [(2 * y + c, 2 * y + 1 - c) for y, c in spots]

    tied = lax.optimization_barrier
    twin = lax.ppermute(own, RING, cross)
    ahead = lax.ppermute(own, RING, along)
    (acc,) = fold(got, [own], None)
    own, acc = tied((own, acc))
    behind = lax.ppermute(own, RING, against)
    (acc,) = fold(got, [twin], acc)
    ahead, acc = tied((ahead, acc))
    ahead_twin = lax.ppermute(ahead, RING, cross)
    (acc,) = fold(got, [ahead], acc)
    ahead, acc = tied((ahead, acc))
    far = lax.ppermute(ahead, RING, along)
    (acc,) = fold(got, [behind], acc)
    behind, acc = tied((behind, acc))
    behind_twin = lax.ppermute(behind, RING, cross)
    (acc,) = fold(got, [ahead_twin], acc)
    far, acc = tied((far, acc))
    far_twin = lax.ppermute(far, RING, cross)
    (acc,) = fold(got, [behind_twin, far], acc)
    every = [own, twin, ahead, behind, ahead_twin, behind_twin, far, far_twin]
    unused, out = fold(got, [far_twin], acc, every)

    back = lax.all_to_all(out, ("x", "z"), 0, 0)
    return finish(back, hidden).reshape(rows_here, cols, chans)


def solution(mesh):
    inner = Mesh(mesh.devices.reshape(NX, NZ, NY, NC, -1), BAND + ("img",))
    place = P(("img",) + BAND, None, None)
    in_specs = (place,) + (P(),) * 9
    return jax.shard_map(
        on_device, mesh=inner, in_specs=in_specs, out_specs=place, check_vma=False
    )
```
